32 devices in a mesh: vox: 8 (over z, y), ch: 4 (over x, core).
Axes of the slice: x: 2, y: 2, z: 4, core: 2. Of those that a mesh axis runs over, the one named last changes fastest.
Arguments:
- features: bfloat16 [8192, 128], P('vox'), may hold values from -6 to 6
- kernel: bfloat16 [27, 256, 128], P(None, 'ch'), may hold values from -0.1875 to 0.1875
- coarse_grad: bfloat16 [256, 4096], P('ch', 'vox'), may hold values from -6 to 6
- pair_fine: int32 [32768], P('vox'), may hold values from 0 to 1023
- pair_target: int32 [32768], P('vox'), may hold values from 0 to 511
- block_offset: int32 [256], P('vox'), may hold values from 0 to 26
- target_owner: int32 [4096, 1], P('vox'), may hold values from 0 to 7; in each aligned block of 512 rows (0 to 511, 512 to 1023, ...) at most 96 rows name the same one
- slot_coarse_row: int32 [6144], P('vox'), may hold values from 0 to 511
- fine_count: int32 [8], P('vox'), may hold values from 512 to 1024, as said below
Outputs:
- activation: bfloat16 [256, 4096], P('ch', 'vox')
- grad_features: bfloat16 [128, 8192], P('ch', 'vox')
- grad_kernel: bfloat16 [27, 256, 128], P(None, 'ch')
The draws below stay inside these ranges and needn't reach their ends.
Inputs may be any that keep to these rules, and one draw needn't show every extreme that they name: `target_owner`: among the 512 targets of one block no owner appears more than 96 times, and in some block one owner appears exactly 96 times. `fine_count`: some block has all 1024 fine voxels live.
All inputs are finite; a program needn't handle non-finite values.
Results may differ from the reference program's by a relative error of at most 0.0053.
Values may be sent and summed in bfloat16 or wider, within the bound.
A program may use at most 64 MiB of HBM per device.

```python
import math
import jax
import jax.numpy as jnp
import numpy as np
from jax import lax

CF = 128
CC = 256
KOFF = 27
FR = 1024
PAIRS = 4096
TG = 512
COARSE_PER_VOXEL = 512
OWNERS = 8
SLOT = 96
NF = 8192
NC = 4096
NPAIRS = 32768
NBLOCKS = 256
TARGETS = 4096
RECEIVE_SLOTS = 6144


def draw_fine_count(key, part):
    first_key, second_key = jax.random.split(jax.random.fold_in(key, 11))
    counts = jax.random.randint(first_key, (OWNERS,), FR // 2, FR + 1)
    chosen = jax.random.randint(second_key, (), 0, OWNERS)
    return jnp.where(jnp.arange(OWNERS) == chosen, FR, counts).astype(jnp.int32)


def place_ends(array, own_key, least, largest):
    dims = array.shape
    place = [jax.random.randint(jax.random.fold_in(own_key, axis), (), 0, dims[axis]) for axis in range(len(dims))]
    array = array.at[tuple(place)].set(least)
    longest = dims.index(max(dims))
    place[longest] = (place[longest] + 1) % dims[longest]
    return array.at[tuple(place)].set(largest)


def shard_levels(rng, dims, cuts, low, largest):
    def one(position, shards_of):
        heights = jax.random.uniform(jax.random.fold_in(jax.random.fold_in(rng, 6), position), (shards_of,), jnp.float32, low / len(cuts), largest / len(cuts))
        return jnp.repeat(jnp.exp(heights), dims[position] // shards_of).reshape((-1,) + (1,) * (len(dims) - position - 1))

    factor_of = one(*cuts[0])
    for cut in cuts[1:]:
        factor_of = factor_of * one(*cut)
    return factor_of


def routed_block(key, own, number, rows, number_of, top, reach, lean):
    order = jax.random.permutation(key, number_of)
    crowded, ordinary = load_shares(number_of, rows * top, reach, lean, True), load_shares(number_of, rows * top, reach, lean, False)
    places = jnp.arange(number_of)

    def named(tallies, turn):
        used = int((tallies > 0).sum())
        fixed = max(1, used // 4)
        shifted = fixed + (places - fixed + turn * (used - fixed)) % max(1, number_of - fixed)
        return jnp.zeros((number_of,), jnp.int32).at[order[jnp.where(places < fixed, places, shifted)]].set(jnp.asarray(tallies, jnp.int32))

    tallies = jnp.where(number % 4 == 0, named(crowded, number // 4), named(ordinary, number - number // 4 - 1))
    mixed = jax.random.permutation(jax.random.fold_in(own, 3), number_of)
    source_of, taker = mixed[0:number_of // 2 * 2:2], mixed[1:number_of // 2 * 2:2]
    room = jnp.minimum(tallies[source_of] - 1, reach - tallies[taker]) // 2
    room = jnp.where((source_of == order[0]) | (taker == order[0]) | (tallies[taker] == 0), 0, jnp.maximum(room, 0))
    shifted = jax.random.randint(jax.random.fold_in(own, 4), (number_of // 2,), 0, 1 << 20) % (room + 1)
    tallies = tallies.at[source_of].add(-shifted).at[taker].add(shifted)
    members = jnp.searchsorted(jnp.cumsum(tallies), jnp.arange(rows * top), side="right").astype(jnp.int32)
    table = members.reshape(top, rows).T
    table = table[jax.random.permutation(jax.random.fold_in(own, 1), rows)]
    turn = jax.random.randint(jax.random.fold_in(own, 2), (rows, 1), 0, top)
    return jnp.take_along_axis(table, (jnp.arange(top)[None, :] + turn) % top, axis=1)


def load_shares(number_of, total, bound, slope, full):
    portions = [(1 << 20) // math.isqrt(standing ** slope) + 1 for standing in range(1, number_of + 1)]
    largest = bound if full else min(bound, max(-(-total // number_of), total * portions[0] // sum(portions)))
    least = 1 if total - largest >= number_of - 1 else 0
    given, spare = [largest] + [least] * (number_of - 1), total - largest - least * (number_of - 1)
    while spare > 0:
        candidates = [i for i in range(1, number_of) if given[i] < largest] or [i for i in range(1, number_of) if given[i] < bound]
        pool, left = sum([portions[i] for i in candidates]), spare
        for i in candidates:
            addition = min(bound - given[i], max(1, left * portions[i] // pool), spare)
            given[i] = given[i] + addition
            spare = spare - addition
    return np.array(given)


def gaussian(own_key, shape, width, limit, cuts=(), kind=jnp.bfloat16):
    values = width * jax.random.normal(own_key, shape, jnp.float32)
    if cuts:
        values = values * shard_levels(own_key, shape, cuts, -0.22, 0.18)
    return jnp.clip(values, -limit, limit).astype(kind)


def setup_inputs(seed: int = 0) -> dict:
    arg_keys = jax.random.split(jax.random.key(seed), 10)
    features = gaussian(arg_keys[0], (NF, CF), 1.0, 6.0, ((0, 8),))
    kernel = gaussian(arg_keys[1], (KOFF, CC, CF), (8 * CF) ** -0.5, 0.1875, ((1, 4),))
    coarse_grad = gaussian(arg_keys[2], (CC, NC), 1.0, 6.0, ((0, 4), (1, 8)))
    pair_fine = place_ends(jax.random.randint(arg_keys[3], (NPAIRS,), 0, FR), jax.random.fold_in(arg_keys[3], 1), 0, FR - 1).astype(jnp.int32)
    pair_target = place_ends(jax.random.randint(arg_keys[4], (NPAIRS,), 0, TG), jax.random.fold_in(arg_keys[4], 1), 0, TG - 1).astype(jnp.int32)
    block_offset = place_ends(jax.random.randint(arg_keys[5], (NBLOCKS,), 0, KOFF), jax.random.fold_in(arg_keys[5], 1), 0, KOFF - 1).astype(jnp.int32)
    target_owner_keys = jax.random.split(jax.random.fold_in(arg_keys[6], 1), TARGETS // TG)
    target_owner_turns = jax.random.permutation(jax.random.fold_in(arg_keys[6], 3), TARGETS // TG)
    target_owner = jax.vmap(lambda own, number: routed_block(jax.random.fold_in(arg_keys[6], 2), own, number, TG, OWNERS, 1, SLOT, 2))(target_owner_keys, target_owner_turns).reshape((TARGETS, 1))
    slot_coarse_row = place_ends(jax.random.randint(arg_keys[7], (RECEIVE_SLOTS,), 0, COARSE_PER_VOXEL), jax.random.fold_in(arg_keys[7], 1), 0, COARSE_PER_VOXEL - 1).astype(jnp.int32)
    fine_count = draw_fine_count(jax.random.fold_in(arg_keys[9], 71), 0)
    return dict(features=features, kernel=kernel, coarse_grad=coarse_grad, pair_fine=pair_fine, pair_target=pair_target, block_offset=block_offset, target_owner=target_owner, slot_coarse_row=slot_coarse_row, fine_count=fine_count)


def owner_slots(owner_of):
    labels = jnp.arange(OWNERS, dtype=jnp.int32)
    onehot = (owner_of[:, None] == labels[None, :]).astype(jnp.int32)
    before = jnp.cumsum(onehot, axis=0) - onehot
    return lax.optimization_barrier(jnp.sum(before * onehot, axis=1)).astype(jnp.int32)

def reference(features, kernel, coarse_grad, pair_fine, pair_target, block_offset, target_owner, slot_coarse_row, fine_count):
    blocks = PAIRS // 128
    live_mask = jnp.arange(FR, dtype=jnp.int32)[None, :] < fine_count[:, None]
    fine = jnp.where(live_mask[:, :, None], features.reshape(OWNERS, FR, CF), jnp.zeros((), features.dtype))
    fine_ids = pair_fine.reshape(OWNERS, PAIRS)
    target_ids = pair_target.reshape(OWNERS, PAIRS)
    offset_ids = block_offset.reshape(OWNERS, blocks)
    owner_of = target_owner.reshape(OWNERS, TG)
    kernel_weight = jnp.transpose(kernel.astype(jnp.float32), (0, 2, 1))

    def forward_one(pieces):
        fine_dev, fine_at, target_at, offset_at = pieces
        gathered = fine_dev[fine_at].astype(jnp.float32).reshape(blocks, 128, CF)
        partial_value = jnp.einsum('bpc,bco->bpo', gathered, kernel_weight[offset_at]).reshape(PAIRS, CC)
        return jax.ops.segment_sum(partial_value, target_at, TG).astype(jnp.bfloat16)
    target_part = lax.map(forward_one, (fine, fine_ids, target_ids, offset_ids))
    slot_of = lax.map(owner_slots, owner_of)
    source = jnp.arange(OWNERS, dtype=jnp.int32)[:, None]
    place_at = owner_of * (OWNERS * SLOT) + source * SLOT + slot_of
    destination = (owner_of * COARSE_PER_VOXEL + slot_coarse_row[place_at]).astype(jnp.int32)
    coarse = jax.ops.segment_sum(target_part.reshape(OWNERS * TG, CC).astype(jnp.float32), destination.reshape(-1), NC)
    gate_output = jax.nn.sigmoid(coarse)
    activation = (coarse * gate_output).astype(jnp.bfloat16)
    grad_coarse = (coarse_grad.astype(jnp.float32).T * gate_output * (1.0 + coarse * (1.0 - gate_output))).astype(jnp.bfloat16)

    def backward_one(reduced_total, pieces):
        fine_dev, fine_at, target_at, offset_at, dest_dev, live_dev = pieces
        gathered = fine_dev[fine_at].astype(jnp.float32).reshape(blocks, 128, CF)
        grad_rows = grad_coarse[dest_dev][target_at].astype(jnp.float32).reshape(blocks, 128, CC)
        grad_in = jnp.einsum('bpo,bco->bpc', grad_rows, kernel_weight[offset_at]).reshape(PAIRS, CF)
        fine_sum = jax.ops.segment_sum(grad_in, fine_at, FR)
        fine_grad = jnp.where(live_dev[:, None], fine_sum, jnp.zeros((), fine_sum.dtype)).astype(jnp.bfloat16)
        grad_weight = jnp.einsum('bpc,bpo->boc', gathered, grad_rows)
        reduced_total = reduced_total + jax.ops.segment_sum(grad_weight, offset_at, KOFF)
        return (reduced_total, fine_grad)
    reduced_total, fine_grads = lax.scan(backward_one, jnp.zeros((KOFF, CC, CF), jnp.float32), (fine, fine_ids, target_ids, offset_ids, destination, live_mask))
    factor = math.sqrt(KOFF / NPAIRS)
    grad_kernel = (reduced_total * factor).astype(jnp.bfloat16)
    return (activation.T, fine_grads.reshape(NF, CF).T, grad_kernel)
```

```python
import functools
import math

import jax
import jax.numpy as jnp
from jax import lax
from jax.experimental import pallas as pl
from jax.experimental.pallas import tpu as pltpu
from jax.sharding import PartitionSpec as P

LANES = 128
NT = (((1,), (1,)), ((), ()))
TN = (((0,), (0,)), ((), ()))
F32 = jnp.float32
BF16 = jnp.bfloat16


def dot(a, b, dims=(((1,), (0,)), ((), ()))):
    return lax.dot_general(a, b, dims, preferred_element_type=F32)


def onehot(rows, ids, base=0):
    at = lax.broadcasted_iota(jnp.int32, (rows, ids.shape[1]), 0) + base
    return (at == ids).astype(BF16)


def onehot_rows(rows, ids_ref, first, count):
    return jnp.concatenate(
        [onehot(rows, ids_ref[pl.ds(first + j, 1), :]) for j in range(count)], axis=1
    )


def split(value):
    high = value.astype(BF16)
    low = (value - high.astype(F32)).astype(BF16)
    return jnp.concatenate([high, low], axis=0)


def joined(value):
    half = value.shape[0] // 2
    return value[:half] + value[half:]


def slots_of(owner_row, owners, padded):
    targets = owner_row.shape[1]
    lead = max(owners, 8)
    mine = onehot(lead, owner_row)
    earlier = lax.broadcasted_iota(jnp.int32, (targets, targets), 0)
    later = lax.broadcasted_iota(jnp.int32, (targets, targets), 1)
    before = dot(mine, (earlier < later).astype(BF16))
    rank = jnp.sum(before * mine.astype(F32), axis=0, keepdims=True)
    return owner_row * padded + rank.astype(jnp.int32)


def forward_kernel(count, feat, ker, pf, pt, off, own, live, send, slot_out, g_out, ft):
    fine_total, width_in = feat.shape
    width_out = ker.shape[1]
    targets = own.shape[1]
    owners, _, padded = send.shape
    rows = pf.shape[0]
    lanes = count * LANES
    at = lax.broadcasted_iota(jnp.int32, (fine_total, width_in), 0)
    masked = jnp.where(at < live[0], feat[...].astype(F32), 0.0)
    ft[...] = masked.T.astype(BF16)

    def group(g, total):
        foh = onehot_rows(fine_total, pf, g * count, count)
        gathered = dot(ft[...], foh).astype(BF16)
        g_out[g] = gathered
        part = jnp.concatenate(
            [
                dot(ker[off[g * count + j]], gathered[:, j * LANES : (j + 1) * LANES])
                for j in range(count)
            ],
            axis=1,
        )
        toh = onehot_rows(targets, pt, g * count, count)
        return total + dot(split(part), toh, NT)

    total = lax.fori_loop(
        0, rows // count, group, jnp.zeros((2 * width_out, targets), F32)
    )
    part = joined(total).astype(BF16)
    slot = slots_of(own[...], owners, padded)
    slot_out[...] = slot

    def route(o, carry):
        send[o] = dot(part, onehot(padded, slot, o * padded), NT).astype(BF16)
        return carry

    lax.fori_loop(0, owners, route, 0)


def middle_kernel(recv, slots, cg, act, back):
    owners = recv.shape[0]
    width_out, coarse_total = cg.shape

    def gather(o, total):
        return total + dot(recv[o], onehot(coarse_total, slots[pl.ds(o, 1), :]), NT)

    coarse = lax.fori_loop(0, owners, gather, jnp.zeros((width_out, coarse_total), F32))
    gate = jax.nn.sigmoid(coarse)
    act[...] = (coarse * gate).astype(BF16)
    grad = (cg[...].astype(F32) * gate * (1.0 + coarse * (1.0 - gate))).astype(BF16)

    def give(o, carry):
        back[o] = dot(grad, onehot(coarse_total, slots[pl.ds(o, 1), :])).astype(BF16)
        return carry

    lax.fori_loop(0, owners, give, 0)


def backward_kernel(count, ret, slot, g_in, ker, pf, pt, off, live, fine, weight, acc):
    owners, width_out, padded = ret.shape
    targets = slot.shape[1]
    width_in, fine_total = fine.shape
    rows = pf.shape[0]

    def gather(o, total):
        return total + dot(ret[o], onehot(padded, slot[...], o * padded))

    grad = lax.fori_loop(
        0, owners, gather, jnp.zeros((width_out, targets), F32)
    ).astype(BF16)
    weight[...] = jnp.zeros_like(weight)
    acc[...] = jnp.zeros_like(acc)

    def group(g, carry):
        toh = onehot_rows(targets, pt, g * count, count)
        spread = dot(grad, toh).astype(BF16)
        gathered = g_in[g]
        parts = []
        for j in range(count):
            k = off[g * count + j]
            mine = spread[:, j * LANES : (j + 1) * LANES]
            weight[k] += dot(mine, gathered[:, j * LANES : (j + 1) * LANES], NT)
            parts.append(dot(ker[k], mine, TN))
        foh = onehot_rows(fine_total, pf, g * count, count)
        acc[...] += dot(split(jnp.concatenate(parts, axis=1)), foh, NT)
        return carry

    lax.fori_loop(0, rows // count, group, 0)
    at = lax.broadcasted_iota(jnp.int32, (width_in, fine_total), 1)
    fine[...] = jnp.where(at < live[0], joined(acc[...]), 0.0)


def body(
    features,
    kernel,
    coarse_grad,
    pair_fine,
    pair_target,
    block_offset,
    target_owner,
    slot_coarse_row,
    fine_count,
):
    owners = lax.axis_size("vox")
    fine_total, width_in = features.shape
    width_out, coarse_total = coarse_grad.shape
    offsets_all = kernel.shape[0]
    targets = target_owner.shape[0]
    capacity = slot_coarse_row.shape[0] // owners
    blocks = block_offset.shape[0]
    padded = -(-capacity // LANES) * LANES
    count = 4
    groups = blocks // count
    vm = pl.BlockSpec(memory_space=pltpu.VMEM)
    sm = pl.BlockSpec(memory_space=pltpu.SMEM)
    params = pltpu.CompilerParams(vmem_limit_bytes=48 * 2**20)
    pf = pair_fine.reshape(blocks, LANES)
    pt = pair_target.reshape(blocks, LANES)
    own = target_owner.reshape(1, targets)
    slots = jnp.pad(
        slot_coarse_row.reshape(owners, capacity),
        ((0, 0), (0, padded - capacity)),
        constant_values=-1,
    )
    exchange = jax.ShapeDtypeStruct((owners, width_out, padded), BF16)
    send, slot, gathered = pl.pallas_call(
        functools.partial(forward_kernel, count),
        out_shape=(
            exchange,
            jax.ShapeDtypeStruct((1, targets), jnp.int32),
            jax.ShapeDtypeStruct((groups, width_in, count * LANES), BF16),
        ),
        in_specs=[vm, vm, vm, vm, sm, vm, sm],
        out_specs=(vm, vm, vm),
        scratch_shapes=[pltpu.VMEM((width_in, fine_total), BF16)],
        compiler_params=params,
    )(features, kernel, pf, pt, block_offset, own, fine_count)
    recv = lax.all_to_all(send, "vox", split_axis=0, concat_axis=0, tiled=True)
    activation, back = pl.pallas_call(
        middle_kernel,
        out_shape=(jax.ShapeDtypeStruct((width_out, coarse_total), BF16), exchange),
        in_specs=[vm, vm, vm],
        out_specs=(vm, vm),
        compiler_params=params,
    )(recv, slots, coarse_grad)
    ret = lax.all_to_all(back, "vox", split_axis=0, concat_axis=0, tiled=True)
    fine_sum, weight_sum = pl.pallas_call(
        functools.partial(backward_kernel, count),
        out_shape=(
            jax.ShapeDtypeStruct((width_in, fine_total), F32),
            jax.ShapeDtypeStruct(kernel.shape, F32),
        ),
        in_specs=[vm, vm, vm, vm, vm, vm, sm, sm],
        out_specs=(vm, vm),
        scratch_shapes=[pltpu.VMEM((2 * width_in, fine_total), F32)],
        compiler_params=params,
    )(ret, slot, gathered, kernel, pf, pt, block_offset, fine_count)
    grad_features = lax.psum_scatter(
        fine_sum, "ch", scatter_dimension=0, tiled=True
    ).astype(BF16)
    factor = math.sqrt(offsets_all / (blocks * LANES * owners))
    grad_kernel = (lax.psum(weight_sum, "vox") * factor).astype(BF16)
    return (activation, grad_features, grad_kernel)


def solution(mesh):
    in_specs = (
        P("vox", None),
        P(None, "ch", None),
        P("ch", "vox"),
        P("vox"),
        P("vox"),
        P("vox"),
        P("vox", None),
        P("vox"),
        P("vox"),
    )
    out_specs = (P("ch", "vox"), P("ch", "vox"), P(None, "ch", None))
    return jax.shard_map(body, mesh=mesh, in_specs=in_specs, out_specs=out_specs, check_vma=False)
```

```python
import functools
import math

import jax
import jax.numpy as jnp
from jax import lax
from jax.experimental import pallas as pl
from jax.experimental.pallas import tpu as pltpu
from jax.sharding import PartitionSpec as P

LANES = 128
MESH = pl.DeviceIdType.MESH
NT = (((1,), (1,)), ((), ()))
TN = (((0,), (0,)), ((), ()))
F32 = jnp.float32
BF16 = jnp.bfloat16


def dot(a, b, dims=(((1,), (0,)), ((), ()))):
    return lax.dot_general(a, b, dims, preferred_element_type=F32)


def onehot(rows, ids, base=0):
    at = lax.broadcasted_iota(jnp.int32, (rows, ids.shape[1]), 0) + base
    return (at == ids).astype(BF16)


def onehot_rows(rows, ids_ref, first, count):
    return jnp.concatenate(
        [onehot(rows, ids_ref[pl.ds(first + j, 1), :]) for j in range(count)], axis=1
    )


def split(value):
    high = value.astype(BF16)
    low = (value - high.astype(F32)).astype(BF16)
    return jnp.concatenate([high, low], axis=0)


def joined(value):
    half = value.shape[0] // 2
    return value[:half] + value[half:]


def slots_of(owner_row, owners, padded):
    targets = owner_row.shape[1]
    lead = max(owners, 8)
    mine = onehot(lead, owner_row)
    earlier = lax.broadcasted_iota(jnp.int32, (targets, targets), 0)
    later = lax.broadcasted_iota(jnp.int32, (targets, targets), 1)
    before = dot(mine, (earlier < later).astype(BF16))
    rank = jnp.sum(before * mine.astype(F32), axis=0, keepdims=True)
    return owner_row * padded + rank.astype(jnp.int32)


def whole_kernel(
    count,
    owners,
    channels,
    factor,
    off,
    live,
    feat_in,
    ker_in,
    cg_in,
    pf_in,
    pt_in,
    own_in,
    slots_in,
    act,
    fine_out,
    weight_out,
    feat,
    ker,
    cg,
    pf,
    pt,
    own,
    slots,
    ft,
    foh,
    toh,
    gath,
    spread,
    send,
    recv,
    back,
    ret,
    prefix,
    links,
    acc,
    fsum,
    fsend,
    frecv,
    wsum,
    wnear,
    wpass,
    wfar,
    wfin,
    in_sem,
    a_send,
    a_recv,
    b_send,
    b_recv,
    f_send,
    f_recv,
    near_send,
    near_recv,
    far_send,
    far_recv,
    out_send,
    out_recv,
    fwd_send,
    fwd_recv,
):
    fine_total, width_in = feat.shape
    offsets_all, width_out, _ = ker.shape
    targets = own.shape[1]
    coarse_total = cg.shape[1]
    padded = send.shape[2]
    blocks = pf.shape[0]
    groups = blocks // count
    slice_rows = wnear.shape[1]
    outer = owners // 2
    vox = lax.axis_index("vox")
    ch = lax.axis_index("ch")
    mine_out, mine_in = vox // 2, lax.rem(vox, 2)

    barrier = pltpu.get_barrier_semaphore()
    for step in range(1, owners):
        pl.semaphore_signal(
            barrier, inc=1, device_id=(lax.rem(vox + step, owners), ch), device_id_type=MESH
        )
    for step in range(1, channels):
        pl.semaphore_signal(
            barrier, inc=1, device_id=(vox, lax.rem(ch + step, channels)), device_id_type=MESH
        )

    pairs = [
        (pf_in, pf),
        (feat_in, feat),
        (pt_in, pt),
        (ker_in, ker),
        (own_in, own),
        (slots_in, slots),
        (cg_in, cg),
    ]
    loads = [pltpu.make_async_copy(a, b, in_sem.at[i]) for i, (a, b) in enumerate(pairs)]
    for load in loads:
        load.start()
    for load in loads[:4]:
        load.wait()

    at = lax.broadcasted_iota(jnp.int32, (fine_total, width_in), 0)
    ft[...] = jnp.where(at < live[0], feat[...].astype(F32), 0.0).T.astype(BF16)

    def forward(g, total):
        foh[g] = onehot_rows(fine_total, pf, g * count, count)
        gathered = dot(ft[...], foh[g]).astype(BF16)
        gath[g] = gathered
        part = jnp.concatenate(
            [
                dot(ker[off[g * count + j]], gathered[:, j * LANES : (j + 1) * LANES])
                for j in range(count)
            ],
            axis=1,
        )
        toh[g] = onehot_rows(targets, pt, g * count, count)
        return total + dot(split(part), toh[g], NT)

    total = lax.fori_loop(0, groups, forward, jnp.zeros((2 * width_out, targets), F32))
    part = joined(total).astype(BF16)
    for load in loads[4:]:
        load.wait()
    slot = slots_of(own[...], owners, padded)

    def route(o, carry):
        send[o] = dot(part, onehot(padded, slot, o * padded), NT).astype(BF16)
        return carry

    lax.fori_loop(0, owners, route, 0, unroll=owners <= 8)

    def exchange(source, target, out_sem, in_sem_of):
        copies = []
        for step in range(1, owners):
            to = lax.rem(vox + step, owners)
            copies.append(
                pltpu.make_async_remote_copy(
                    src_ref=source.at[to],
                    dst_ref=target.at[vox],
                    send_sem=out_sem.at[step],
                    recv_sem=in_sem_of.at[step],
                    device_id=(to, ch),
                    device_id_type=MESH,
                )
            )
            copies[-1].start()
        target[vox] = source[vox]
        return copies

    pl.semaphore_wait(barrier, owners - 1 + channels - 1)
    copies = exchange(send, recv, a_send, a_recv)

    def link(b, carry):
        found = jnp.int32(0)
        for other in range(blocks):
            same = jnp.logical_and(off[other] == off[b], other < b)
            found = jnp.where(same, jnp.int32(other + 1), found)
        links[b] = found
        return carry

    def ending(k, carry):
        found = jnp.int32(0)
        for other in range(blocks):
            found = jnp.where(off[other] == k, jnp.int32(other + 1), found)
        links[blocks + k] = found
        return carry

    lax.fori_loop(0, blocks, link, 0)
    lax.fori_loop(0, offsets_all, ending, 0)
    for copy in copies:
        copy.wait()

    def gather(o, total):
        return total + dot(recv[o], onehot(coarse_total, slots[pl.ds(o, 1), :]), NT)

    coarse = lax.fori_loop(
        0, owners, gather, jnp.zeros((width_out, coarse_total), F32), unroll=owners <= 8
    )
    gate = jax.nn.sigmoid(coarse)
    act[...] = (coarse * gate).astype(BF16)
    grad = (cg[...].astype(F32) * gate * (1.0 + coarse * (1.0 - gate))).astype(BF16)

    def give(o, carry):
        back[o] = dot(grad, onehot(coarse_total, slots[pl.ds(o, 1), :])).astype(BF16)
        return carry

    lax.fori_loop(0, owners, give, 0, unroll=owners <= 8)
    copies = exchange(back, ret, b_send, b_recv)
    acc[...] = jnp.zeros_like(acc)
    prefix[0] = jnp.zeros_like(prefix[0])
    wsum[...] = jnp.zeros_like(wsum)
    for copy in copies:
        copy.wait()

    def take(o, total):
        return total + dot(ret[o], onehot(padded, slot, o * padded))

    grad = lax.fori_loop(
        0, owners, take, jnp.zeros((width_out, targets), F32), unroll=owners <= 8
    ).astype(BF16)

    def weigh(g, carry):
        rows = dot(grad, toh[g]).astype(BF16)
        spread[g] = rows
        gathered = gath[g]
        for j in range(count):
            lanes = slice(j * LANES, (j + 1) * LANES)
            b = g * count + j
            prefix[b + 1] = prefix[links[b]] + dot(rows[:, lanes], gathered[:, lanes], NT)
        return carry

    lax.fori_loop(0, groups, weigh, 0)

    def pick(k, carry):
        rows = pl.ds(pl.multiple_of(k * width_out, width_out), width_out)
        wsum[rows, :] = prefix[links[blocks + k]].astype(BF16)
        return carry

    lax.fori_loop(0, offsets_all, pick, 0)

    def slice_of(out_at, in_at):
        first = (out_at * 2 + in_at) * slice_rows
        return pl.ds(pl.multiple_of(first, 16), slice_rows)

    partner = mine_out * 2 + 1 - mine_in
    order = list(range(1, outer)) + [0]
    near = {}
    for step in order:
        to = lax.rem(mine_out + step, outer)
        near[step] = pltpu.make_async_remote_copy(
            src_ref=wsum.at[slice_of(to, 1 - mine_in)],
            dst_ref=wnear.at[step],
            send_sem=near_send.at[step],
            recv_sem=near_recv.at[step],
            device_id=(partner, ch),
            device_id_type=MESH,
        )
        near[step].start()

    def scatter(g, carry):
        parts = []
        for j in range(count):
            k = off[g * count + j]
            parts.append(dot(ker[k], spread[g, :, j * LANES : (j + 1) * LANES], TN))
        acc[...] += dot(split(jnp.concatenate(parts, axis=1)), foh[g], NT)
        return carry

    far = {}
    done = 0
    for number, step in enumerate(order):
        until = groups * (number + 1) // outer
        if until > done:
            lax.fori_loop(done, until, scatter, 0)
            done = until
        to = lax.rem(mine_out + step, outer)
        near[step].wait()
        both = wsum[slice_of(to, mine_in), :].astype(F32) + wnear[step].astype(F32)
        if step == 0:
            total = both
        else:
            wpass[step] = both.astype(BF16)
            far[step] = pltpu.make_async_remote_copy(
                src_ref=wpass.at[step],
                dst_ref=wfar.at[step],
                send_sem=far_send.at[step],
                recv_sem=far_recv.at[step],
                device_id=(to * 2 + mine_in, ch),
                device_id_type=MESH,
            )
            far[step].start()

    share = width_in // channels
    mask_at = lax.broadcasted_iota(jnp.int32, (width_in, fine_total), 1)
    whole = jnp.where(mask_at < live[0], joined(acc[...]), 0.0)
    fsum[...] = whole
    fsend[...] = whole.astype(BF16)
    fine = []
    for step in range(1, channels):
        to = lax.rem(ch + step, channels)
        fine.append(
            pltpu.make_async_remote_copy(
                src_ref=fsend.at[pl.ds(pl.multiple_of(to * share, share), share)],
                dst_ref=frecv.at[step],
                send_sem=f_send.at[step],
                recv_sem=f_recv.at[step],
                device_id=(vox, to),
                device_id_type=MESH,
            )
        )
        fine[-1].start()

    for step in order[:-1]:
        far[step].wait()
        total = total + wfar[step].astype(F32)
    here = slice_of(mine_out, mine_in)
    wfin[here, :] = (total * factor).astype(BF16)

    def finished(where, to, out_sem, in_sem_of):
        copy = pltpu.make_async_remote_copy(
            src_ref=wfin.at[where],
            dst_ref=wfin.at[where],
            send_sem=out_sem,
            recv_sem=in_sem_of,
            device_id=(to, ch),
            device_id_type=MESH,
        )
        copy.start()
        return copy

    outward = [
        finished(
            here,
            lax.rem(mine_out + step, outer) * 2 + mine_in,
            out_send.at[step],
            out_recv.at[step],
        )
        for step in range(1, outer)
    ]
    across = [finished(here, partner, fwd_send.at[0], fwd_recv.at[0])]

    for copy in fine:
        copy.wait()
    kept = fsum[pl.ds(pl.multiple_of(ch * share, share), share), :]
    for step in range(1, channels):
        kept = kept + frecv[step].astype(F32)
    fine_out[...] = kept.astype(BF16)

    for step in range(1, outer):
        outward[step - 1].wait()
        came = slice_of(lax.rem(mine_out + outer - step, outer), mine_in)
        across.append(finished(came, partner, fwd_send.at[step], fwd_recv.at[step]))
    for copy in across:
        copy.wait()

    def deliver(k, carry):
        rows = pl.ds(pl.multiple_of(k * width_out, width_out), width_out)
        weight_out[k] = wfin[rows, :]
        return carry

    lax.fori_loop(0, offsets_all, deliver, 0)


def body(
    features,
    kernel,
    coarse_grad,
    pair_fine,
    pair_target,
    block_offset,
    target_owner,
    slot_coarse_row,
    fine_count,
):
    owners = lax.axis_size("vox")
    channels = lax.axis_size("ch")
    fine_total, width_in = features.shape
    width_out, coarse_total = coarse_grad.shape
    offsets_all = kernel.shape[0]
    targets = target_owner.shape[0]
    capacity = slot_coarse_row.shape[0] // owners
    blocks = block_offset.shape[0]
    padded = -(-capacity // LANES) * LANES
    count = 4
    groups = blocks // count
    outer = owners // 2
    slice_rows = -(-offsets_all * width_out // (owners * 16)) * 16
    share = width_in // channels
    vm = pl.BlockSpec(memory_space=pltpu.VMEM)
    sm = pl.BlockSpec(memory_space=pltpu.SMEM)
    hbm = pl.BlockSpec(memory_space=pl.ANY)
    pf = pair_fine.reshape(blocks, LANES)
    pt = pair_target.reshape(blocks, LANES)
    own = target_owner.reshape(1, targets)
    slots = jnp.pad(
        slot_coarse_row.reshape(owners, capacity),
        ((0, 0), (0, padded - capacity)),
        constant_values=-1,
    )
    factor = math.sqrt(offsets_all / (blocks * LANES * owners))
    operands = (features, kernel, coarse_grad, pf, pt, own, slots)
    wide = count * LANES
    dma = pltpu.SemaphoreType.DMA
    scratch = [pltpu.VMEM(a.shape, a.dtype) for a in operands] + [
        pltpu.VMEM((width_in, fine_total), BF16),
        pltpu.VMEM((groups, fine_total, wide), BF16),
        pltpu.VMEM((groups, targets, wide), BF16),
        pltpu.VMEM((groups, width_in, wide), BF16),
        pltpu.VMEM((groups, width_out, wide), BF16),
        pltpu.VMEM((owners, width_out, padded), BF16),
        pltpu.VMEM((owners, width_out, padded), BF16),
        pltpu.VMEM((owners, width_out, padded), BF16),
        pltpu.VMEM((owners, width_out, padded), BF16),
        pltpu.VMEM((blocks + 1, width_out, width_in), F32),
        pltpu.SMEM((blocks + offsets_all,), jnp.int32),
        pltpu.VMEM((2 * width_in, fine_total), F32),
        pltpu.VMEM((width_in, fine_total), F32),
        pltpu.VMEM((width_in, fine_total), BF16),
        pltpu.VMEM((channels, share, fine_total), BF16),
        pltpu.VMEM((owners * slice_rows, width_in), BF16),
        pltpu.VMEM((outer, slice_rows, width_in), BF16),
        pltpu.VMEM((outer, slice_rows, width_in), BF16),
        pltpu.VMEM((outer, slice_rows, width_in), BF16),
        pltpu.VMEM((owners * slice_rows, width_in), BF16),
        dma((len(operands),)),
        dma((owners,)),
        dma((owners,)),
        dma((owners,)),
        dma((owners,)),
        dma((channels,)),
        dma((channels,)),
    ] + [dma((outer,)) for _ in range(8)]
    return pl.pallas_call(
        functools.partial(whole_kernel, count, owners, channels, factor),
        out_shape=(
            jax.ShapeDtypeStruct((width_out, coarse_total), BF16),
            jax.ShapeDtypeStruct((share, fine_total), BF16),
            jax.ShapeDtypeStruct(kernel.shape, BF16),
        ),
        in_specs=[sm, sm] + [hbm] * len(operands),
        out_specs=(vm, vm, vm),
        scratch_shapes=scratch,
        compiler_params=pltpu.CompilerParams(
            collective_id=0, has_side_effects=True, vmem_limit_bytes=50 * 2**20
        ),
    )(block_offset, fine_count, *operands)


def solution(mesh):
    in_specs = (
        P("vox", None),
        P(None, "ch", None),
        P("ch", "vox"),
        P("vox"),
        P("vox"),
        P("vox"),
        P("vox", None),
        P("vox"),
        P("vox"),
    )
    out_specs = (P("ch", "vox"), P("ch", "vox"), P(None, "ch", None))
    return jax.shard_map(body, mesh=mesh, in_specs=in_specs, out_specs=out_specs, check_vma=False)
```

```python
import functools
import math

import jax
import jax.numpy as jnp
from jax import lax
from jax.experimental import pallas as pl
from jax.experimental.pallas import tpu as pltpu
from jax.sharding import PartitionSpec as P

LANES = 128
MESH = pl.DeviceIdType.MESH
NT = (((1,), (1,)), ((), ()))
TN = (((0,), (0,)), ((), ()))
F32 = jnp.float32
BF16 = jnp.bfloat16


def dot(a, b, dims=(((1,), (0,)), ((), ()))):
    return lax.dot_general(a, b, dims, preferred_element_type=F32)


def onehot(rows, ids, base=0):
    at = lax.broadcasted_iota(jnp.int32, (rows, ids.shape[1]), 0).astype(jnp.int16)
    wanted = jnp.clip(ids - base, -1, rows).astype(jnp.int16)
    one = jnp.ones(at.shape, BF16)
    return jnp.where(at == wanted, one, jnp.zeros_like(one))


def onehot_rows(rows, ids_ref, first, count):
    return jnp.concatenate(
        [onehot(rows, ids_ref[pl.ds(first + j, 1), :]) for j in range(count)], axis=1
    )


def split(value):
    high = value.astype(BF16)
    low = (value - high.astype(F32)).astype(BF16)
    return jnp.concatenate([high, low], axis=0)


def joined(value):
    half = value.shape[0] // 2
    return value[:half] + value[half:]


def slots_of(owner_row, owners, padded):
    targets = owner_row.shape[1]
    lead = max(owners, 8)
    mine = onehot(lead, owner_row)
    earlier = lax.broadcasted_iota(jnp.int32, (targets, targets), 0)
    later = lax.broadcasted_iota(jnp.int32, (targets, targets), 1)
    before = dot(mine, (earlier < later).astype(BF16))
    rank = jnp.sum(before * mine.astype(F32), axis=0, keepdims=True)
    return owner_row * padded + rank.astype(jnp.int32)


def whole_kernel(
    count,
    owners,
    channels,
    factor,
    off,
    live,
    feat_in,
    ker_in,
    cg_in,
    pf_in,
    pt_in,
    own_in,
    slots_in,
    act_out,
    fine_out,
    weight_out,
    act,
    fine_here,
    feat,
    ker,
    cg,
    pf,
    pt,
    own,
    slots,
    routes,
    places,
    ft,
    foh,
    toh,
    gath,
    spread,
    send,
    recv,
    back,
    ret,
    prefix,
    links,
    acc,
    fsum,
    fsend,
    frecv,
    wsum,
    wnear,
    wpass,
    wfar,
    wfin,
    in_sem,
    end_sem,
    a_send,
    a_recv,
    b_send,
    b_recv,
    f_send,
    f_recv,
    near_send,
    near_recv,
    far_send,
    far_recv,
    out_send,
    out_recv,
    fwd_send,
    fwd_recv,
):
    fine_total, width_in = feat.shape
    offsets_all, width_out, _ = ker.shape
    targets = own.shape[1]
    coarse_total = cg.shape[1]
    padded = send.shape[2]
    blocks = pf.shape[0]
    groups = blocks // count
    slice_rows = wnear.shape[1]
    outer = owners // 2
    vox = lax.axis_index("vox")
    ch = lax.axis_index("ch")
    mine_out, mine_in = vox // 2, lax.rem(vox, 2)

    barrier = pltpu.get_barrier_semaphore()
    for step in range(1, owners):
        pl.semaphore_signal(
            barrier, inc=1, device_id=(lax.rem(vox + step, owners), ch), device_id_type=MESH
        )
    for step in range(1, channels):
        pl.semaphore_signal(
            barrier, inc=1, device_id=(vox, lax.rem(ch + step, channels)), device_id_type=MESH
        )

    pairs = [
        (own_in, own),
        (slots_in, slots),
        (pf_in, pf),
        (pt_in, pt),
        (feat_in, feat),
        (ker_in, ker),
        (cg_in, cg),
    ]
    loads = [pltpu.make_async_copy(a, b, in_sem.at[i]) for i, (a, b) in enumerate(pairs)]
    for load in loads:
        load.start()
    small = owners <= 16
    for load in loads[:2]:
        load.wait()
    slot = slots_of(own[...], owners, padded)
    if small:
        routes[...] = onehot(owners * padded, slot)
        capacity = slots.shape[0] * LANES // owners
        blank = jnp.full((1, padded - capacity), -1, jnp.int32)
        for o in range(owners):
            pieces, first = [], o * capacity
            while first < (o + 1) * capacity:
                row, lane = divmod(first, LANES)
                size = min(LANES - lane, (o + 1) * capacity - first)
                pieces.append(slots[row : row + 1, lane : lane + size])
                first += size
            if padded > capacity:
                pieces.append(blank)
            ids = jnp.concatenate(pieces, axis=1)
            places[:, o * padded : (o + 1) * padded] = onehot(coarse_total, ids)
    for load in loads[2:6]:
        load.wait()

    at = lax.broadcasted_iota(jnp.int32, (fine_total, width_in), 0)
    ft[...] = jnp.where(at < live[0], feat[...].astype(F32), 0.0).T.astype(BF16)

    def forward(g, total):
        foh[g] = onehot_rows(fine_total, pf, g * count, count)
        gathered = dot(ft[...], foh[g]).astype(BF16)
        gath[g] = gathered
        part = jnp.concatenate(
            [
                dot(ker[off[g * count + j]], gathered[:, j * LANES : (j + 1) * LANES])
                for j in range(count)
            ],
            axis=1,
        )
        toh[g] = onehot_rows(targets, pt, g * count, count)
        return total + dot(split(part), toh[g], NT)

    total = lax.fori_loop(
        0, groups, forward, jnp.zeros((2 * width_out, targets), F32), unroll=True
    )
    part = joined(total).astype(BF16)

    def route(o, carry):
        send[o] = dot(part, onehot(padded, slot, o * padded), NT).astype(BF16)
        return carry

    def apart(value, target):
        for o in range(owners):
            target[o] = value[:, o * padded : (o + 1) * padded].astype(BF16)

    def together(source):
        return jnp.concatenate([source[o] for o in range(owners)], axis=1)

    if small:
        apart(dot(part, routes[...], NT), send)
    else:
        lax.fori_loop(0, owners, route, 0)
    loads[6].wait()

    def exchange(source, target, out_sem, in_sem_of):
        copies = []
        for step in range(1, owners):
            to = lax.rem(vox + step, owners)
            copies.append(
                pltpu.make_async_remote_copy(
                    src_ref=source.at[to],
                    dst_ref=target.at[vox],
                    send_sem=out_sem.at[step],
                    recv_sem=in_sem_of.at[step],
                    device_id=(to, ch),
                    device_id_type=MESH,
                )
            )
            copies[-1].start()
        target[vox] = source[vox]
        return copies

    pl.semaphore_wait(barrier, owners - 1 + channels - 1)
    copies = exchange(send, recv, a_send, a_recv)

    def link(b, carry):
        found = jnp.int32(0)
        for other in range(blocks):
            same = jnp.logical_and(off[other] == off[b], other < b)
            found = jnp.where(same, jnp.int32(other + 1), found)
        links[b] = found
        return carry

    def ending(k, carry):
        found = jnp.int32(0)
        for other in range(blocks):
            found = jnp.where(off[other] == k, jnp.int32(other + 1), found)
        links[blocks + k] = found
        return carry

    lax.fori_loop(0, blocks, link, 0)
    lax.fori_loop(0, offsets_all, ending, 0)
    for copy in copies:
        copy.wait()

    def gather(o, total):
        return total + dot(recv[o], onehot(coarse_total, slots[pl.ds(o, 1), :]), NT)

    if small:
        coarse = dot(together(recv), places[...], NT)
    else:
        coarse = lax.fori_loop(0, owners, gather, jnp.zeros(cg.shape, F32))
    gate = jax.nn.sigmoid(coarse)
    act[...] = (coarse * gate).astype(BF16)
    stores = [pltpu.make_async_copy(act, act_out, end_sem.at[0])]
    stores[-1].start()
    grad = (cg[...].astype(F32) * gate * (1.0 + coarse * (1.0 - gate))).astype(BF16)

    def give(o, carry):
        back[o] = dot(grad, onehot(coarse_total, slots[pl.ds(o, 1), :])).astype(BF16)
        return carry

    if small:
        apart(dot(grad, places[...]), back)
    else:
        lax.fori_loop(0, owners, give, 0)
    copies = exchange(back, ret, b_send, b_recv)
    acc[...] = jnp.zeros_like(acc)
    prefix[0] = jnp.zeros_like(prefix[0])
    wsum[...] = jnp.zeros_like(wsum)
    for copy in copies:
        copy.wait()

    def take(o, total):
        return total + dot(ret[o], onehot(padded, slot, o * padded))

    if small:
        grad = dot(together(ret), routes[...]).astype(BF16)
    else:
        grad = lax.fori_loop(
            0, owners, take, jnp.zeros((width_out, targets), F32)
        ).astype(BF16)

    def weigh(g, carry):
        rows = dot(grad, toh[g]).astype(BF16)
        spread[g] = rows
        gathered = gath[g]
        for j in range(count):
            lanes = slice(j * LANES, (j + 1) * LANES)
            b = g * count + j
            prefix[b + 1] = prefix[links[b]] + dot(rows[:, lanes], gathered[:, lanes], NT)
        return carry

    lax.fori_loop(0, groups, weigh, 0, unroll=True)

    def pick(k, carry):
        rows = pl.ds(pl.multiple_of(k * width_out, width_out), width_out)
        wsum[rows, :] = prefix[links[blocks + k]].astype(BF16)
        return carry

    lax.fori_loop(0, offsets_all, pick, 0)

    def slice_of(out_at, in_at):
        first = (out_at * 2 + in_at) * slice_rows
        return pl.ds(pl.multiple_of(first, 16), slice_rows)

    partner = mine_out * 2 + 1 - mine_in
    order = list(range(1, outer)) + [0]
    near = {}
    for step in order:
        to = lax.rem(mine_out + step, outer)
        near[step] = pltpu.make_async_remote_copy(
            src_ref=wsum.at[slice_of(to, 1 - mine_in)],
            dst_ref=wnear.at[step],
            send_sem=near_send.at[step],
            recv_sem=near_recv.at[step],
            device_id=(partner, ch),
            device_id_type=MESH,
        )
        near[step].start()

    def scatter(g, carry):
        parts = []
        for j in range(count):
            k = off[g * count + j]
            parts.append(dot(ker[k], spread[g, :, j * LANES : (j + 1) * LANES], TN))
        acc[...] += dot(split(jnp.concatenate(parts, axis=1)), foh[g], NT)
        return carry

    far = {}
    done = 0
    for number, step in enumerate(order):
        until = groups * (number + 1) // outer
        if until > done:
            lax.fori_loop(done, until, scatter, 0, unroll=True)
            done = until
        to = lax.rem(mine_out + step, outer)
        near[step].wait()
        both = wsum[slice_of(to, mine_in), :].astype(F32) + wnear[step].astype(F32)
        if step == 0:
            total = both
        else:
            wpass[step] = both.astype(BF16)
            far[step] = pltpu.make_async_remote_copy(
                src_ref=wpass.at[step],
                dst_ref=wfar.at[step],
                send_sem=far_send.at[step],
                recv_sem=far_recv.at[step],
                device_id=(to * 2 + mine_in, ch),
                device_id_type=MESH,
            )
            far[step].start()

    share = width_in // channels
    mask_at = lax.broadcasted_iota(jnp.int32, (width_in, fine_total), 1)
    whole = jnp.where(mask_at < live[0], joined(acc[...]), 0.0)
    fsum[...] = whole
    fsend[...] = whole.astype(BF16)
    fine = []
    for step in range(1, channels):
        to = lax.rem(ch + step, channels)
        fine.append(
            pltpu.make_async_remote_copy(
                src_ref=fsend.at[pl.ds(pl.multiple_of(to * share, share), share)],
                dst_ref=frecv.at[step],
                send_sem=f_send.at[step],
                recv_sem=f_recv.at[step],
                device_id=(vox, to),
                device_id_type=MESH,
            )
        )
        fine[-1].start()

    for step in order[:-1]:
        far[step].wait()
        total = total + wfar[step].astype(F32)
    here = slice_of(mine_out, mine_in)
    wfin[here, :] = (total * factor).astype(BF16)

    def finished(where, to, out_sem, in_sem_of):
        copy = pltpu.make_async_remote_copy(
            src_ref=wfin.at[where],
            dst_ref=wfin.at[where],
            send_sem=out_sem,
            recv_sem=in_sem_of,
            device_id=(to, ch),
            device_id_type=MESH,
        )
        copy.start()
        return copy

    outward = [
        finished(
            here,
            lax.rem(mine_out + step, outer) * 2 + mine_in,
            out_send.at[step],
            out_recv.at[step],
        )
        for step in range(1, outer)
    ]
    across = [finished(here, partner, fwd_send.at[0], fwd_recv.at[0])]

    for copy in fine:
        copy.wait()
    kept = fsum[pl.ds(pl.multiple_of(ch * share, share), share), :]
    for step in range(1, channels):
        kept = kept + frecv[step].astype(F32)
    fine_here[...] = kept.astype(BF16)
    stores.append(pltpu.make_async_copy(fine_here, fine_out, end_sem.at[1]))
    stores[-1].start()

    for step in range(1, outer):
        outward[step - 1].wait()
        came = slice_of(lax.rem(mine_out + outer - step, outer), mine_in)
        across.append(finished(came, partner, fwd_send.at[step], fwd_recv.at[step]))
    for copy in across:
        copy.wait()

    rows = offsets_all * width_out
    stores.append(
        pltpu.make_async_copy(wfin.at[pl.ds(0, rows)], weight_out, end_sem.at[2])
    )
    stores[-1].start()
    for copy in stores:
        copy.wait()


def write_kernel(a, b, c, a_out, b_out, c_out, sem):
    pairs = ((c, c_out), (a, a_out), (b, b_out))
    copies = [pltpu.make_async_copy(x, y, sem.at[i]) for i, (x, y) in enumerate(pairs)]
    for copy in copies:
        copy.start()
    for copy in copies:
        copy.wait()


def body(
    features,
    kernel,
    coarse_grad,
    pair_fine,
    pair_target,
    block_offset,
    target_owner,
    slot_coarse_row,
    fine_count,
):
    owners = lax.axis_size("vox")
    channels = lax.axis_size("ch")
    fine_total, width_in = features.shape
    width_out, coarse_total = coarse_grad.shape
    offsets_all = kernel.shape[0]
    targets = target_owner.shape[0]
    capacity = slot_coarse_row.shape[0] // owners
    blocks = block_offset.shape[0]
    padded = -(-capacity // LANES) * LANES
    count = 4
    groups = blocks // count
    outer = owners // 2
    slice_rows = -(-offsets_all * width_out // (owners * 16)) * 16
    share = width_in // channels
    sm = pl.BlockSpec(memory_space=pltpu.SMEM)
    hbm = pl.BlockSpec(memory_space=pltpu.HBM)
    pf = pair_fine.reshape(blocks, LANES)
    pt = pair_target.reshape(blocks, LANES)
    own = target_owner.reshape(1, targets)
    small = owners <= 16
    if small:
        slots = slot_coarse_row.reshape(-1, LANES)
    else:
        slots = jnp.pad(
            slot_coarse_row.reshape(owners, capacity),
            ((0, 0), (0, padded - capacity)),
            constant_values=-1,
        )
    kept = owners * padded if small else LANES
    factor = math.sqrt(offsets_all / (blocks * LANES * owners))
    operands = (features, kernel, coarse_grad, pf, pt, own, slots)
    wide = count * LANES
    dma = pltpu.SemaphoreType.DMA
    shapes = (
        jax.ShapeDtypeStruct((width_out, coarse_total), BF16),
        jax.ShapeDtypeStruct((share, fine_total), BF16),
        jax.ShapeDtypeStruct(kernel.shape, BF16),
    )
    scratch = [pltpu.VMEM(a.shape, BF16) for a in shapes[:2]]
    scratch += [pltpu.VMEM(a.shape, a.dtype) for a in operands] + [
        pltpu.VMEM((kept, targets), BF16),
        pltpu.VMEM((coarse_total, kept), BF16),
        pltpu.VMEM((width_in, fine_total), BF16),
        pltpu.VMEM((groups, fine_total, wide), BF16),
        pltpu.VMEM((groups, targets, wide), BF16),
        pltpu.VMEM((groups, width_in, wide), BF16),
        pltpu.VMEM((groups, width_out, wide), BF16),
        pltpu.VMEM((owners, width_out, padded), BF16),
        pltpu.VMEM((owners, width_out, padded), BF16),
        pltpu.VMEM((owners, width_out, padded), BF16),
        pltpu.VMEM((owners, width_out, padded), BF16),
        pltpu.VMEM((blocks + 1, width_out, width_in), F32),
        pltpu.SMEM((blocks + offsets_all,), jnp.int32),
        pltpu.VMEM((2 * width_in, fine_total), F32),
        pltpu.VMEM((width_in, fine_total), F32),
        pltpu.VMEM((width_in, fine_total), BF16),
        pltpu.VMEM((channels, share, fine_total), BF16),
        pltpu.VMEM((owners * slice_rows, width_in), BF16),
        pltpu.VMEM((outer, slice_rows, width_in), BF16),
        pltpu.VMEM((outer, slice_rows, width_in), BF16),
        pltpu.VMEM((outer, slice_rows, width_in), BF16),
        pltpu.VMEM((owners * slice_rows, width_in), BF16),
        dma((len(operands),)),
        dma((3,)),
        dma((owners,)),
        dma((owners,)),
        dma((owners,)),
        dma((owners,)),
        dma((channels,)),
        dma((channels,)),
    ] + [dma((outer,)) for _ in range(8)]
    results = pl.pallas_call(
        functools.partial(whole_kernel, count, owners, channels, factor),
        out_shape=shapes[:2]
        + (jax.ShapeDtypeStruct((offsets_all * width_out, width_in), BF16),),
        in_specs=[sm, sm] + [hbm] * len(operands),
        out_specs=(hbm, hbm, hbm),
        scratch_shapes=scratch,
        compiler_params=pltpu.CompilerParams(
            collective_id=0, has_side_effects=True, vmem_limit_bytes=60 * 2**20
        ),
    )(block_offset, fine_count, *operands)
    return pl.pallas_call(
        write_kernel,
        out_shape=shapes,
        in_specs=[hbm, hbm, hbm],
        out_specs=(hbm, hbm, hbm),
        scratch_shapes=[dma((3,))],
        compiler_params=pltpu.CompilerParams(vmem_limit_bytes=60 * 2**20),
    )(results[0], results[1], results[2].reshape(kernel.shape))


def solution(mesh):
    in_specs = (
        P("vox", None),
        P(None, "ch", None),
        P("ch", "vox"),
        P("vox"),
        P("vox"),
        P("vox"),
        P("vox", None),
        P("vox"),
        P("vox"),
    )
    out_specs = (P("ch", "vox"), P("ch", "vox"), P(None, "ch", None))
    return jax.shard_map(body, mesh=mesh, in_specs=in_specs, out_specs=out_specs, check_vma=False)
```

```python
import functools
import math

import jax
import jax.numpy as jnp
from jax import lax
from jax.experimental import pallas as pl
from jax.experimental.pallas import tpu as pltpu
from jax.sharding import PartitionSpec as P

LANES = 128
MESH = pl.DeviceIdType.MESH
NT = (((1,), (1,)), ((), ()))
TN = (((0,), (0,)), ((), ()))
F32 = jnp.float32
BF16 = jnp.bfloat16


def dot(a, b, dims=(((1,), (0,)), ((), ()))):
    return lax.dot_general(a, b, dims, preferred_element_type=F32)


def onehot(rows, ids, base=0):
    at = lax.broadcasted_iota(jnp.int32, (rows, ids.shape[1]), 0).astype(jnp.int16)
    wanted = jnp.clip(ids - base, -1, rows).astype(jnp.int16)
    one = jnp.ones(at.shape, BF16)
    return jnp.where(at == wanted, one, jnp.zeros_like(one))


def onehot_rows(rows, ids_ref, first, count):
    return jnp.concatenate(
        [onehot(rows, ids_ref[pl.ds(first + j, 1), :]) for j in range(count)], axis=1
    )


def split(value):
    high = value.astype(BF16)
    low = (value - high.astype(F32)).astype(BF16)
    return jnp.concatenate([high, low], axis=0)


def joined(value):
    half = value.shape[0] // 2
    return value[:half] + value[half:]


def slots_of(owner_row, owners, padded):
    targets = owner_row.shape[1]
    lead = max(owners, 8)
    mine = onehot(lead, owner_row)
    earlier = lax.broadcasted_iota(jnp.int32, (targets, targets), 0)
    later = lax.broadcasted_iota(jnp.int32, (targets, targets), 1)
    before = dot(mine, (earlier < later).astype(BF16))
    rank = jnp.sum(before * mine.astype(F32), axis=0, keepdims=True)
    return owner_row * padded + rank.astype(jnp.int32)


def whole_kernel(
    count,
    owners,
    channels,
    factor,
    off,
    live,
    feat_in,
    ker_in,
    cg_in,
    pf_in,
    pt_in,
    own_in,
    slots_in,
    act_out,
    fine_out,
    weight_out,
    act,
    fine_here,
    feat,
    ker,
    cg,
    pf,
    pt,
    own,
    slots,
    routes,
    places,
    ft,
    foh,
    toh,
    gath,
    spread,
    send,
    recv,
    back,
    ret,
    prefix,
    links,
    acc,
    fsum,
    fsend,
    frecv,
    wsum,
    wnear,
    wpass,
    wfar,
    wfin,
    in_sem,
    end_sem,
    a_send,
    a_recv,
    b_send,
    b_recv,
    f_send,
    f_recv,
    near_send,
    near_recv,
    far_send,
    far_recv,
    out_send,
    out_recv,
    fwd_send,
    fwd_recv,
):
    fine_total, width_in = feat.shape
    offsets_all, width_out, _ = ker.shape
    targets = own.shape[1]
    coarse_total = cg.shape[1]
    padded = send.shape[2]
    blocks = pf.shape[0]
    groups = blocks // count
    slice_rows = wfin.shape[0] // owners
    outer = owners // 2
    vox = lax.axis_index("vox")
    ch = lax.axis_index("ch")
    mine_out, mine_in = vox // 2, lax.rem(vox, 2)

    barrier = pltpu.get_barrier_semaphore()
    for step in range(1, owners):
        pl.semaphore_signal(
            barrier, inc=1, device_id=(lax.rem(vox + step, owners), ch), device_id_type=MESH
        )
    for step in range(1, channels):
        pl.semaphore_signal(
            barrier, inc=1, device_id=(vox, lax.rem(ch + step, channels)), device_id_type=MESH
        )

    pairs = [
        (own_in, own),
        (slots_in, slots),
        (pf_in, pf),
        (pt_in, pt),
        (feat_in, feat),
        (ker_in, ker),
        (cg_in, cg),
    ]
    loads = [pltpu.make_async_copy(a, b, in_sem.at[i]) for i, (a, b) in enumerate(pairs)]
    for load in loads:
        load.start()
    small = owners <= 16
    for load in loads[:2]:
        load.wait()
    slot = slots_of(own[...], owners, padded)
    if small:
        routes[...] = onehot(owners * padded, slot)
        capacity = slots.shape[0] * LANES // owners
        blank = jnp.full((1, padded - capacity), -1, jnp.int32)
        for o in range(owners):
            pieces, first = [], o * capacity
            while first < (o + 1) * capacity:
                row, lane = divmod(first, LANES)
                size = min(LANES - lane, (o + 1) * capacity - first)
                pieces.append(slots[row : row + 1, lane : lane + size])
                first += size
            if padded > capacity:
                pieces.append(blank)
            ids = jnp.concatenate(pieces, axis=1)
            places[:, o * padded : (o + 1) * padded] = onehot(coarse_total, ids)
    for load in loads[2:6]:
        load.wait()

    at = lax.broadcasted_iota(jnp.int32, (fine_total, width_in), 0)
    ft[...] = jnp.where(at < live[0], feat[...].astype(F32), 0.0).T.astype(BF16)

    def forward(g, total):
        foh[g] = onehot_rows(fine_total, pf, g * count, count)
        gathered = dot(ft[...], foh[g]).astype(BF16)
        gath[g] = gathered
        part = jnp.concatenate(
            [
                dot(ker[off[g * count + j]], gathered[:, j * LANES : (j + 1) * LANES])
                for j in range(count)
            ],
            axis=1,
        )
        toh[g] = onehot_rows(targets, pt, g * count, count)
        return total + dot(split(part), toh[g], NT)

    total = lax.fori_loop(
        0, groups, forward, jnp.zeros((2 * width_out, targets), F32), unroll=True
    )
    part = joined(total).astype(BF16)

    def route(o, carry):
        send[o] = dot(part, onehot(padded, slot, o * padded), NT).astype(BF16)
        return carry

    def apart(value, target):
        for o in range(owners):
            target[o] = value[:, o * padded : (o + 1) * padded].astype(BF16)

    def together(source):
        return jnp.concatenate([source[o] for o in range(owners)], axis=1)

    if small:
        apart(dot(part, routes[...], NT), send)
    else:
        lax.fori_loop(0, owners, route, 0)
    loads[6].wait()

    def exchange(source, target, out_sem, in_sem_of):
        copies = []
        for step in range(1, owners):
            to = lax.rem(vox + step, owners)
            copies.append(
                pltpu.make_async_remote_copy(
                    src_ref=source.at[to],
                    dst_ref=target.at[vox],
                    send_sem=out_sem.at[step],
                    recv_sem=in_sem_of.at[step],
                    device_id=(to, ch),
                    device_id_type=MESH,
                )
            )
            copies[-1].start()
        target[vox] = source[vox]
        return copies

    pl.semaphore_wait(barrier, owners - 1 + channels - 1)
    copies = exchange(send, recv, a_send, a_recv)

    def link(b, carry):
        found = jnp.int32(0)
        for other in range(blocks):
            same = jnp.logical_and(off[other] == off[b], other < b)
            found = jnp.where(same, jnp.int32(other + 1), found)
        links[b] = found
        return carry

    def ending(k, carry):
        found = jnp.int32(0)
        for other in range(blocks):
            found = jnp.where(off[other] == k, jnp.int32(other + 1), found)
        links[blocks + k] = found
        return carry

    lax.fori_loop(0, blocks, link, 0)
    for copy in copies:
        copy.wait()

    def gather(o, total):
        return total + dot(recv[o], onehot(coarse_total, slots[pl.ds(o, 1), :]), NT)

    if small:
        coarse = dot(together(recv), places[...], NT)
    else:
        coarse = lax.fori_loop(0, owners, gather, jnp.zeros(cg.shape, F32))
    gate = jax.nn.sigmoid(coarse)
    act[...] = (coarse * gate).astype(BF16)
    stores = [pltpu.make_async_copy(act, act_out, end_sem.at[0])]
    stores[-1].start()
    grad = (cg[...].astype(F32) * gate * (1.0 + coarse * (1.0 - gate))).astype(BF16)

    def give(o, carry):
        back[o] = dot(grad, onehot(coarse_total, slots[pl.ds(o, 1), :])).astype(BF16)
        return carry

    if small:
        apart(dot(grad, places[...]), back)
    else:
        lax.fori_loop(0, owners, give, 0)
    copies = exchange(back, ret, b_send, b_recv)
    acc[...] = jnp.zeros_like(acc)
    prefix[0] = jnp.zeros_like(prefix[0])
    wsum[...] = jnp.zeros_like(wsum)
    lax.fori_loop(0, offsets_all, ending, 0)
    for copy in copies:
        copy.wait()

    def take(o, total):
        return total + dot(ret[o], onehot(padded, slot, o * padded))

    if small:
        grad = dot(together(ret), routes[...]).astype(BF16)
    else:
        grad = lax.fori_loop(
            0, owners, take, jnp.zeros((width_out, targets), F32)
        ).astype(BF16)

    def weigh(g, carry):
        rows = dot(grad, toh[g]).astype(BF16)
        spread[g] = rows
        gathered = gath[g]
        for j in range(count):
            lanes = slice(j * LANES, (j + 1) * LANES)
            b = g * count + j
            prefix[b + 1] = prefix[links[b]] + dot(rows[:, lanes], gathered[:, lanes], NT)
        return carry

    lax.fori_loop(0, groups, weigh, 0, unroll=True)

    def pick(k, carry):
        rows = pl.ds(pl.multiple_of(k * width_out, width_out), width_out)
        wsum[rows, :] = prefix[links[blocks + k]].astype(BF16)
        return carry

    lax.fori_loop(0, offsets_all, pick, 0, unroll=True)

    part_rows = wnear.shape[2]
    parts = slice_rows // part_rows

    def piece(out_at, in_at, part):
        first = (out_at * 2 + in_at) * slice_rows + part * part_rows
        return pl.ds(pl.multiple_of(first, 16), part_rows)

    partner = mine_out * 2 + 1 - mine_in
    order = list(range(1, outer)) + [0]
    near = {}
    for part in range(parts):
        for step in order:
            to = lax.rem(mine_out + step, outer)
            near[part, step] = pltpu.make_async_remote_copy(
                src_ref=wsum.at[piece(to, 1 - mine_in, part)],
                dst_ref=wnear.at[part, step],
                send_sem=near_send.at[part, step],
                recv_sem=near_recv.at[part, step],
                device_id=(partner, ch),
                device_id_type=MESH,
            )
            near[part, step].start()

    def scatter(g, carry):
        terms = []
        for j in range(count):
            k = off[g * count + j]
            terms.append(dot(ker[k], spread[g, :, j * LANES : (j + 1) * LANES], TN))
        acc[...] += dot(split(jnp.concatenate(terms, axis=1)), foh[g], NT)
        return carry

    far, totals = {}, {}

    def pass_on(part, step):
        to = lax.rem(mine_out + step, outer)
        near[part, step].wait()
        both = wsum[piece(to, mine_in, part), :].astype(F32)
        both = both + wnear[part, step].astype(F32)
        if step == 0:
            totals[part] = both
            return
        wpass[part, step] = both.astype(BF16)
        far[part, step] = pltpu.make_async_remote_copy(
            src_ref=wpass.at[part, step],
            dst_ref=wfar.at[part, step],
            send_sem=far_send.at[part, step],
            recv_sem=far_recv.at[part, step],
            device_id=(to * 2 + mine_in, ch),
            device_id_type=MESH,
        )
        far[part, step].start()

    done = 0
    for number, step in enumerate(order):
        until = groups * (number + 1) // outer
        if until > done:
            lax.fori_loop(done, until, scatter, 0, unroll=True)
            done = until
        pass_on(0, step)
    for part in range(1, parts):
        for step in order:
            pass_on(part, step)

    share = width_in // channels
    mask_at = lax.broadcasted_iota(jnp.int32, (width_in, fine_total), 1)
    whole = jnp.where(mask_at < live[0], joined(acc[...]), 0.0)
    fsum[...] = whole
    fsend[...] = whole.astype(BF16)
    fine = []
    for step in range(1, channels):
        to = lax.rem(ch + step, channels)
        fine.append(
            pltpu.make_async_remote_copy(
                src_ref=fsend.at[pl.ds(pl.multiple_of(to * share, share), share)],
                dst_ref=frecv.at[step],
                send_sem=f_send.at[step],
                recv_sem=f_recv.at[step],
                device_id=(vox, to),
                device_id_type=MESH,
            )
        )
        fine[-1].start()

    def finished(where, to, out_sem, in_sem_of):
        copy = pltpu.make_async_remote_copy(
            src_ref=wfin.at[where],
            dst_ref=wfin.at[where],
            send_sem=out_sem,
            recv_sem=in_sem_of,
            device_id=(to, ch),
            device_id_type=MESH,
        )
        copy.start()
        return copy

    outward, across = {}, []
    for part in range(parts):
        total = totals[part]
        for step in order[:-1]:
            far[part, step].wait()
            total = total + wfar[part, step].astype(F32)
        here = piece(mine_out, mine_in, part)
        wfin[here, :] = (total * factor).astype(BF16)
        for step in range(1, outer):
            outward[part, step] = finished(
                here,
                lax.rem(mine_out + step, outer) * 2 + mine_in,
                out_send.at[part, step],
                out_recv.at[part, step],
            )
        across.append(
            finished(here, partner, fwd_send.at[part, 0], fwd_recv.at[part, 0])
        )

    def forward_on(part):
        for step in range(1, outer):
            outward[part, step].wait()
            came = piece(lax.rem(mine_out + outer - step, outer), mine_in, part)
            across.append(
                finished(
                    came, partner, fwd_send.at[part, step], fwd_recv.at[part, step]
                )
            )

    forward_on(0)
    for copy in fine:
        copy.wait()
    kept = fsum[pl.ds(pl.multiple_of(ch * share, share), share), :]
    for step in range(1, channels):
        kept = kept + frecv[step].astype(F32)
    fine_here[...] = kept.astype(BF16)
    stores.append(pltpu.make_async_copy(fine_here, fine_out, end_sem.at[1]))
    stores[-1].start()
    for part in range(1, parts):
        forward_on(part)
    for copy in across:
        copy.wait()

    rows = offsets_all * width_out
    stores.append(
        pltpu.make_async_copy(wfin.at[pl.ds(0, rows)], weight_out, end_sem.at[2])
    )
    stores[-1].start()
    for copy in stores:
        copy.wait()


def body(
    features,
    kernel,
    coarse_grad,
    pair_fine,
    pair_target,
    block_offset,
    target_owner,
    slot_coarse_row,
    fine_count,
):
    owners = lax.axis_size("vox")
    channels = lax.axis_size("ch")
    fine_total, width_in = features.shape
    width_out, coarse_total = coarse_grad.shape
    offsets_all = kernel.shape[0]
    targets = target_owner.shape[0]
    capacity = slot_coarse_row.shape[0] // owners
    blocks = block_offset.shape[0]
    padded = -(-capacity // LANES) * LANES
    count = 4
    groups = blocks // count
    outer = owners // 2
    slice_rows = -(-offsets_all * width_out // (owners * 16)) * 16
    parts = 2 if slice_rows % 32 == 0 else 1
    share = width_in // channels
    sm = pl.BlockSpec(memory_space=pltpu.SMEM)
    hbm = pl.BlockSpec(memory_space=pltpu.HBM)
    pf = pair_fine.reshape(blocks, LANES)
    pt = pair_target.reshape(blocks, LANES)
    own = target_owner.reshape(1, targets)
    small = owners <= 16
    if small:
        slots = slot_coarse_row.reshape(-1, LANES)
    else:
        slots = jnp.pad(
            slot_coarse_row.reshape(owners, capacity),
            ((0, 0), (0, padded - capacity)),
            constant_values=-1,
        )
    kept = owners * padded if small else LANES
    factor = math.sqrt(offsets_all / (blocks * LANES * owners))
    operands = (features, kernel, coarse_grad, pf, pt, own, slots)
    wide = count * LANES
    dma = pltpu.SemaphoreType.DMA
    shapes = (
        jax.ShapeDtypeStruct((width_out, coarse_total), BF16),
        jax.ShapeDtypeStruct((share, fine_total), BF16),
        jax.ShapeDtypeStruct(kernel.shape, BF16),
    )
    scratch = [pltpu.VMEM(a.shape, BF16) for a in shapes[:2]]
    scratch += [pltpu.VMEM(a.shape, a.dtype) for a in operands] + [
        pltpu.VMEM((kept, targets), BF16),
        pltpu.VMEM((coarse_total, kept), BF16),
        pltpu.VMEM((width_in, fine_total), BF16),
        pltpu.VMEM((groups, fine_total, wide), BF16),
        pltpu.VMEM((groups, targets, wide), BF16),
        pltpu.VMEM((groups, width_in, wide), BF16),
        pltpu.VMEM((groups, width_out, wide), BF16),
        pltpu.VMEM((owners, width_out, padded), BF16),
        pltpu.VMEM((owners, width_out, padded), BF16),
        pltpu.VMEM((owners, width_out, padded), BF16),
        pltpu.VMEM((owners, width_out, padded), BF16),
        pltpu.VMEM((blocks + 1, width_out, width_in), F32),
        pltpu.SMEM((blocks + offsets_all,), jnp.int32),
        pltpu.VMEM((2 * width_in, fine_total), F32),
        pltpu.VMEM((width_in, fine_total), F32),
        pltpu.VMEM((width_in, fine_total), BF16),
        pltpu.VMEM((channels, share, fine_total), BF16),
        pltpu.VMEM((owners * slice_rows, width_in), BF16),
        pltpu.VMEM((parts, outer, slice_rows // parts, width_in), BF16),
        pltpu.VMEM((parts, outer, slice_rows // parts, width_in), BF16),
        pltpu.VMEM((parts, outer, slice_rows // parts, width_in), BF16),
        pltpu.VMEM((owners * slice_rows, width_in), BF16),
        dma((len(operands),)),
        dma((3,)),
        dma((owners,)),
        dma((owners,)),
        dma((owners,)),
        dma((owners,)),
        dma((channels,)),
        dma((channels,)),
    ] + [dma((parts, outer)) for _ in range(8)]
    results = pl.pallas_call(
        functools.partial(whole_kernel, count, owners, channels, factor),
        out_shape=shapes[:2]
        + (jax.ShapeDtypeStruct((offsets_all * width_out, width_in), BF16),),
        in_specs=[sm, sm] + [hbm] * len(operands),
        out_specs=(hbm, hbm, hbm),
        scratch_shapes=scratch,
        compiler_params=pltpu.CompilerParams(
            collective_id=0, has_side_effects=True, vmem_limit_bytes=60 * 2**20
        ),
    )(block_offset, fine_count, *operands)
    return (results[0], results[1], results[2].reshape(kernel.shape))


def solution(mesh):
    in_specs = (
        P("vox", None),
        P(None, "ch", None),
        P("ch", "vox"),
        P("vox"),
        P("vox"),
        P("vox"),
        P("vox", None),
        P("vox"),
        P("vox"),
    )
    out_specs = (P("ch", "vox"), P("ch", "vox"), P(None, "ch", None))
    return jax.shard_map(body, mesh=mesh, in_specs=in_specs, out_specs=out_specs, check_vma=False)
```

```python
import functools
import math

import jax
import jax.numpy as jnp
from jax import lax
from jax.experimental import pallas as pl
from jax.experimental.pallas import tpu as pltpu
from jax.sharding import PartitionSpec as P

LANES = 128
MESH = pl.DeviceIdType.MESH
NT = (((1,), (1,)), ((), ()))
TN = (((0,), (0,)), ((), ()))
F32 = jnp.float32
BF16 = jnp.bfloat16


def dot(a, b, dims=(((1,), (0,)), ((), ()))):
    return lax.dot_general(a, b, dims, preferred_element_type=F32)


def onehot(rows, ids, base=0):
    at = lax.broadcasted_iota(jnp.int32, (rows, ids.shape[1]), 0).astype(jnp.int16)
    wanted = jnp.clip(ids - base, -1, rows).astype(jnp.int16)
    one = jnp.ones(at.shape, BF16)
    return jnp.where(at == wanted, one, jnp.zeros_like(one))


def onehot_rows(rows, ids_ref, first, count):
    return jnp.concatenate(
        [onehot(rows, ids_ref[pl.ds(first + j, 1), :]) for j in range(count)], axis=1
    )


def split(value):
    high = value.astype(BF16)
    low = (value - high.astype(F32)).astype(BF16)
    return jnp.concatenate([high, low], axis=0)


def joined(value):
    half = value.shape[0] // 2
    return value[:half] + value[half:]


def slots_of(owner_row, owners, padded):
    targets = owner_row.shape[1]
    lead = max(owners, 8)
    mine = onehot(lead, owner_row)
    earlier = lax.broadcasted_iota(jnp.int32, (targets, targets), 0)
    later = lax.broadcasted_iota(jnp.int32, (targets, targets), 1)
    before = dot(mine, (earlier < later).astype(BF16))
    rank = jnp.sum(before * mine.astype(F32), axis=0, keepdims=True)
    return owner_row * padded + rank.astype(jnp.int32)


def whole_kernel(
    count,
    owners,
    channels,
    factor,
    off,
    live,
    feat_in,
    ker_in,
    cg_in,
    pf_in,
    pt_in,
    own_in,
    slots_in,
    act_out,
    fine_out,
    weight_out,
    act,
    fine_here,
    feat,
    ker,
    cg,
    pf,
    pt,
    own,
    slots,
    routes,
    places,
    ft,
    foh,
    toh,
    gath,
    spread,
    send,
    recv,
    back,
    ret,
    prefix,
    links,
    acc,
    fsum,
    fsend,
    frecv,
    wsum,
    wnear,
    wpass,
    wfar,
    wfin,
    in_sem,
    end_sem,
    a_send,
    a_recv,
    b_send,
    b_recv,
    f_send,
    f_recv,
    near_send,
    near_recv,
    far_send,
    far_recv,
    out_send,
    out_recv,
    fwd_send,
    fwd_recv,
):
    fine_total, width_in = feat.shape
    offsets_all, width_out, _ = ker.shape
    targets = own.shape[1]
    coarse_total = cg.shape[1]
    padded = send.shape[2]
    blocks = pf.shape[0]
    groups = blocks // count
    slice_rows = wfin.shape[0] // owners
    outer = owners // 2
    vox = lax.axis_index("vox")
    ch = lax.axis_index("ch")
    mine_out, mine_in = vox // 2, lax.rem(vox, 2)

    barrier = pltpu.get_barrier_semaphore()
    for step in range(1, owners):
        pl.semaphore_signal(
            barrier, inc=1, device_id=(lax.rem(vox + step, owners), ch), device_id_type=MESH
        )
    for step in range(1, channels):
        pl.semaphore_signal(
            barrier, inc=1, device_id=(vox, lax.rem(ch + step, channels)), device_id_type=MESH
        )

    pairs = [
        (own_in, own),
        (slots_in, slots),
        (pf_in, pf),
        (pt_in, pt),
        (feat_in, feat),
        (ker_in, ker),
        (cg_in, cg),
    ]
    loads = [pltpu.make_async_copy(a, b, in_sem.at[i]) for i, (a, b) in enumerate(pairs)]
    for load in loads:
        load.start()
    small = owners <= 16
    for load in loads[:2]:
        load.wait()
    slot = slots_of(own[...], owners, padded)
    if small:
        routes[...] = onehot(owners * padded, slot)
        capacity = slots.shape[0] * LANES // owners
        blank = jnp.full((1, padded - capacity), -1, jnp.int32)
        for o in range(owners):
            pieces, first = [], o * capacity
            while first < (o + 1) * capacity:
                row, lane = divmod(first, LANES)
                size = min(LANES - lane, (o + 1) * capacity - first)
                pieces.append(slots[row : row + 1, lane : lane + size])
                first += size
            if padded > capacity:
                pieces.append(blank)
            ids = jnp.concatenate(pieces, axis=1)
            places[:, o * padded : (o + 1) * padded] = onehot(coarse_total, ids)
    for load in loads[2:6]:
        load.wait()

    at = lax.broadcasted_iota(jnp.int32, (fine_total, width_in), 0)
    ft[...] = jnp.where(at < live[0], feat[...].astype(F32), 0.0).T.astype(BF16)

    def forward(g, total):
        foh[g] = onehot_rows(fine_total, pf, g * count, count)
        gathered = dot(ft[...], foh[g]).astype(BF16)
        gath[g] = gathered
        part = jnp.concatenate(
            [
                dot(ker[off[g * count + j]], gathered[:, j * LANES : (j + 1) * LANES])
                for j in range(count)
            ],
            axis=1,
        )
        toh[g] = onehot_rows(targets, pt, g * count, count)
        return total + dot(split(part), toh[g], NT)

    total = lax.fori_loop(
        0, groups, forward, jnp.zeros((2 * width_out, targets), F32), unroll=True
    )
    part = joined(total).astype(BF16)

    def route(o, carry):
        send[o] = dot(part, onehot(padded, slot, o * padded), NT).astype(BF16)
        return carry

    def apart(value, target):
        for o in range(owners):
            target[o] = value[:, o * padded : (o + 1) * padded].astype(BF16)

    def together(source):
        return jnp.concatenate([source[o] for o in range(owners)], axis=1)

    if small:
        apart(dot(part, routes[...], NT), send)
    else:
        lax.fori_loop(0, owners, route, 0)
    loads[6].wait()

    def exchange(source, target, out_sem, in_sem_of):
        copies = []
        for step in range(1, owners):
            to = lax.rem(vox + step, owners)
            copies.append(
                pltpu.make_async_remote_copy(
                    src_ref=source.at[to],
                    dst_ref=target.at[vox],
                    send_sem=out_sem.at[step],
                    recv_sem=in_sem_of.at[step],
                    device_id=(to, ch),
                    device_id_type=MESH,
                )
            )
            copies[-1].start()
        target[vox] = source[vox]
        return copies

    pl.semaphore_wait(barrier, owners - 1 + channels - 1)
    copies = exchange(send, recv, a_send, a_recv)

    def link(b, carry):
        found = jnp.int32(0)
        for other in range(blocks):
            same = jnp.logical_and(off[other] == off[b], other < b)
            found = jnp.where(same, jnp.int32(other + 1), found)
        links[b] = found
        return carry

    def ending(k, carry):
        found = jnp.int32(0)
        for other in range(blocks):
            found = jnp.where(off[other] == k, jnp.int32(other + 1), found)
        links[blocks + k] = found
        return carry

    lax.fori_loop(0, blocks, link, 0)
    for copy in copies:
        copy.wait()

    def gather(o, total):
        return total + dot(recv[o], onehot(coarse_total, slots[pl.ds(o, 1), :]), NT)

    if small:
        coarse = dot(together(recv), places[...], NT)
    else:
        coarse = lax.fori_loop(0, owners, gather, jnp.zeros(cg.shape, F32))
    gate = jax.nn.sigmoid(coarse)
    act[...] = (coarse * gate).astype(BF16)
    stores = [pltpu.make_async_copy(act, act_out, end_sem.at[0])]
    stores[-1].start()
    grad = (cg[...].astype(F32) * gate * (1.0 + coarse * (1.0 - gate))).astype(BF16)

    def give(o, carry):
        back[o] = dot(grad, onehot(coarse_total, slots[pl.ds(o, 1), :])).astype(BF16)
        return carry

    if small:
        apart(dot(grad, places[...]), back)
    else:
        lax.fori_loop(0, owners, give, 0)
    copies = exchange(back, ret, b_send, b_recv)
    prefix[0] = jnp.zeros_like(prefix[0])
    wsum[...] = jnp.zeros_like(wsum)
    lax.fori_loop(0, offsets_all, ending, 0)
    for copy in copies:
        copy.wait()

    def take(o, total):
        return total + dot(ret[o], onehot(padded, slot, o * padded))

    if small:
        grad = dot(together(ret), routes[...]).astype(BF16)
    else:
        grad = lax.fori_loop(
            0, owners, take, jnp.zeros((width_out, targets), F32)
        ).astype(BF16)

    def weigh(g, carry):
        rows = dot(grad, toh[g]).astype(BF16)
        spread[g] = rows
        gathered = gath[g]
        for j in range(count):
            lanes = slice(j * LANES, (j + 1) * LANES)
            b = g * count + j
            prefix[b + 1] = prefix[links[b]] + dot(rows[:, lanes], gathered[:, lanes], NT)
        return carry

    lax.fori_loop(0, groups, weigh, 0, unroll=True)

    def pick(k, carry):
        rows = pl.ds(pl.multiple_of(k * width_out, width_out), width_out)
        wsum[rows, :] = prefix[links[blocks + k]].astype(BF16)
        return carry

    lax.fori_loop(0, offsets_all, pick, 0, unroll=True)

    part_rows = wnear.shape[2]
    parts = slice_rows // part_rows

    def piece(out_at, in_at, part):
        first = (out_at * 2 + in_at) * slice_rows + part * part_rows
        return pl.ds(pl.multiple_of(first, 16), part_rows)

    partner = mine_out * 2 + 1 - mine_in
    order = list(range(1, outer)) + [0]
    near = {}
    for part in range(parts):
        for step in order:
            to = lax.rem(mine_out + step, outer)
            near[part, step] = pltpu.make_async_remote_copy(
                src_ref=wsum.at[piece(to, 1 - mine_in, part)],
                dst_ref=wnear.at[part, step],
                send_sem=near_send.at[part, step],
                recv_sem=near_recv.at[part, step],
                device_id=(partner, ch),
                device_id_type=MESH,
            )
            near[part, step].start()

    pace = 2 if groups % 2 == 0 else 1

    def scatter(turn):
        more = None
        for g in range(turn * pace, (turn + 1) * pace):
            terms = []
            for j in range(count):
                rows = spread[g, :, j * LANES : (j + 1) * LANES]
                terms.append(dot(ker[off[g * count + j]], rows, TN).astype(BF16))
            added = dot(jnp.concatenate(terms, axis=1), foh[g], NT)
            more = added if more is None else more + added
        acc[...] = more if turn == 0 else acc[...] + more

    far, totals = {}, {}

    def pass_on(part, step):
        to = lax.rem(mine_out + step, outer)
        near[part, step].wait()
        both = wsum[piece(to, mine_in, part), :].astype(F32)
        both = both + wnear[part, step].astype(F32)
        if step == 0:
            totals[part] = both
            return
        wpass[part, step] = both.astype(BF16)
        far[part, step] = pltpu.make_async_remote_copy(
            src_ref=wpass.at[part, step],
            dst_ref=wfar.at[part, step],
            send_sem=far_send.at[part, step],
            recv_sem=far_recv.at[part, step],
            device_id=(to * 2 + mine_in, ch),
            device_id_type=MESH,
        )
        far[part, step].start()

    turns = groups // pace
    scatter(0)
    for step in order[:-1]:
        pass_on(0, step)
    if turns > 1:
        scatter(1)
    pass_on(0, 0)
    for part in range(1, parts):
        for step in order:
            pass_on(part, step)
    for turn in range(2, turns - 1):
        scatter(turn)

    def finished(where, to, out_sem, in_sem_of):
        copy = pltpu.make_async_remote_copy(
            src_ref=wfin.at[where],
            dst_ref=wfin.at[where],
            send_sem=out_sem,
            recv_sem=in_sem_of,
            device_id=(to, ch),
            device_id_type=MESH,
        )
        copy.start()
        return copy

    outward, across = {}, []

    def finish(part):
        total = totals[part]
        for step in order[:-1]:
            far[part, step].wait()
            total = total + wfar[part, step].astype(F32)
        here = piece(mine_out, mine_in, part)
        wfin[here, :] = (total * factor).astype(BF16)
        for step in range(1, outer):
            outward[part, step] = finished(
                here,
                lax.rem(mine_out + step, outer) * 2 + mine_in,
                out_send.at[part, step],
                out_recv.at[part, step],
            )
        across.append(
            finished(here, partner, fwd_send.at[part, 0], fwd_recv.at[part, 0])
        )

    for part in range(parts):
        finish(part)
    if turns > 2:
        scatter(turns - 1)

    share = width_in // channels
    mask_at = lax.broadcasted_iota(jnp.int32, (width_in, fine_total), 1)
    whole = jnp.where(mask_at < live[0], acc[...], 0.0)
    fsum[...] = whole
    fsend[...] = whole.astype(BF16)
    fine = []
    for step in range(1, channels):
        to = lax.rem(ch + step, channels)
        fine.append(
            pltpu.make_async_remote_copy(
                src_ref=fsend.at[pl.ds(pl.multiple_of(to * share, share), share)],
                dst_ref=frecv.at[step],
                send_sem=f_send.at[step],
                recv_sem=f_recv.at[step],
                device_id=(vox, to),
                device_id_type=MESH,
            )
        )
        fine[-1].start()

    def forward_on(part):
        for step in range(1, outer):
            outward[part, step].wait()
            came = piece(lax.rem(mine_out + outer - step, outer), mine_in, part)
            across.append(
                finished(
                    came, partner, fwd_send.at[part, step], fwd_recv.at[part, step]
                )
            )

    forward_on(0)
    for copy in fine:
        copy.wait()
    kept = fsum[pl.ds(pl.multiple_of(ch * share, share), share), :]
    for step in range(1, channels):
        kept = kept + frecv[step].astype(F32)
    fine_here[...] = kept.astype(BF16)
    stores.append(pltpu.make_async_copy(fine_here, fine_out, end_sem.at[1]))
    stores[-1].start()
    for part in range(1, parts):
        forward_on(part)
    for copy in across:
        copy.wait()

    rows = offsets_all * width_out
    stores.append(
        pltpu.make_async_copy(wfin.at[pl.ds(0, rows)], weight_out, end_sem.at[2])
    )
    stores[-1].start()
    for copy in stores:
        copy.wait()


def write_kernel(a, b, c, a_out, b_out, c_out, a_mid, b_mid, c_mid, in_sem, out_sem):
    pairs = ((c, c_mid, c_out), (a, a_mid, a_out), (b, b_mid, b_out))
    loads = [pltpu.make_async_copy(p[0], p[1], in_sem.at[i]) for i, p in enumerate(pairs)]
    stores = [pltpu.make_async_copy(p[1], p[2], out_sem.at[i]) for i, p in enumerate(pairs)]
    for load in loads:
        load.start()
    for load, store in zip(loads, stores):
        load.wait()
        store.start()
    for store in stores:
        store.wait()


def body(
    features,
    kernel,
    coarse_grad,
    pair_fine,
    pair_target,
    block_offset,
    target_owner,
    slot_coarse_row,
    fine_count,
):
    owners = lax.axis_size("vox")
    channels = lax.axis_size("ch")
    fine_total, width_in = features.shape
    width_out, coarse_total = coarse_grad.shape
    offsets_all = kernel.shape[0]
    targets = target_owner.shape[0]
    capacity = slot_coarse_row.shape[0] // owners
    blocks = block_offset.shape[0]
    padded = -(-capacity // LANES) * LANES
    count = 4
    groups = blocks // count
    outer = owners // 2
    slice_rows = -(-offsets_all * width_out // (owners * 16)) * 16
    parts = 2 if slice_rows % 32 == 0 else 1
    share = width_in // channels
    sm = pl.BlockSpec(memory_space=pltpu.SMEM)
    hbm = pl.BlockSpec(memory_space=pltpu.HBM)
    pf = pair_fine.reshape(blocks, LANES)
    pt = pair_target.reshape(blocks, LANES)
    own = target_owner.reshape(1, targets)
    small = owners <= 16
    if small:
        slots = slot_coarse_row.reshape(-1, LANES)
    else:
        slots = jnp.pad(
            slot_coarse_row.reshape(owners, capacity),
            ((0, 0), (0, padded - capacity)),
            constant_values=-1,
        )
    kept = owners * padded if small else LANES
    factor = math.sqrt(offsets_all / (blocks * LANES * owners))
    operands = (features, kernel, coarse_grad, pf, pt, own, slots)
    wide = count * LANES
    dma = pltpu.SemaphoreType.DMA
    shapes = (
        jax.ShapeDtypeStruct((width_out, coarse_total), BF16),
        jax.ShapeDtypeStruct((share, fine_total), BF16),
        jax.ShapeDtypeStruct(kernel.shape, BF16),
    )
    scratch = [pltpu.VMEM(a.shape, BF16) for a in shapes[:2]]
    scratch += [pltpu.VMEM(a.shape, a.dtype) for a in operands] + [
        pltpu.VMEM((kept, targets), BF16),
        pltpu.VMEM((coarse_total, kept), BF16),
        pltpu.VMEM((width_in, fine_total), BF16),
        pltpu.VMEM((groups, fine_total, wide), BF16),
        pltpu.VMEM((groups, targets, wide), BF16),
        pltpu.VMEM((groups, width_in, wide), BF16),
        pltpu.VMEM((groups, width_out, wide), BF16),
        pltpu.VMEM((owners, width_out, padded), BF16),
        pltpu.VMEM((owners, width_out, padded), BF16),
        pltpu.VMEM((owners, width_out, padded), BF16),
        pltpu.VMEM((owners, width_out, padded), BF16),
        pltpu.VMEM((blocks + 1, width_out, width_in), F32),
        pltpu.SMEM((blocks + offsets_all,), jnp.int32),
        pltpu.VMEM((width_in, fine_total), F32),
        pltpu.VMEM((width_in, fine_total), F32),
        pltpu.VMEM((width_in, fine_total), BF16),
        pltpu.VMEM((channels, share, fine_total), BF16),
        pltpu.VMEM((owners * slice_rows, width_in), BF16),
        pltpu.VMEM((parts, outer, slice_rows // parts, width_in), BF16),
        pltpu.VMEM((parts, outer, slice_rows // parts, width_in), BF16),
        pltpu.VMEM((parts, outer, slice_rows // parts, width_in), BF16),
        pltpu.VMEM((owners * slice_rows, width_in), BF16),
        dma((len(operands),)),
        dma((3,)),
        dma((owners,)),
        dma((owners,)),
        dma((owners,)),
        dma((owners,)),
        dma((channels,)),
        dma((channels,)),
    ] + [dma((parts, outer)) for _ in range(8)]
    results = pl.pallas_call(
        functools.partial(whole_kernel, count, owners, channels, factor),
        out_shape=shapes[:2]
        + (jax.ShapeDtypeStruct((offsets_all * width_out, width_in), BF16),),
        in_specs=[sm, sm] + [hbm] * len(operands),
        out_specs=(hbm, hbm, hbm),
        scratch_shapes=scratch,
        compiler_params=pltpu.CompilerParams(
            collective_id=0, has_side_effects=True, vmem_limit_bytes=60 * 2**20
        ),
    )(block_offset, fine_count, *operands)
    return pl.pallas_call(
        write_kernel,
        out_shape=shapes,
        in_specs=[hbm, hbm, hbm],
        out_specs=(hbm, hbm, hbm),
        scratch_shapes=[pltpu.VMEM(a.shape, BF16) for a in shapes] + [dma((3,)), dma((3,))],
        compiler_params=pltpu.CompilerParams(vmem_limit_bytes=60 * 2**20),
    )(results[0], results[1], results[2].reshape(kernel.shape))


def solution(mesh):
    in_specs = (
        P("vox", None),
        P(None, "ch", None),
        P("ch", "vox"),
        P("vox"),
        P("vox"),
        P("vox"),
        P("vox", None),
        P("vox"),
        P("vox"),
    )
    out_specs = (P("ch", "vox"), P("ch", "vox"), P(None, "ch", None))
    return jax.shard_map(body, mesh=mesh, in_specs=in_specs, out_specs=out_specs, check_vma=False)
```

```python
import functools
import math

import jax
import jax.numpy as jnp
from jax import lax
from jax.experimental import pallas as pl
from jax.experimental.pallas import tpu as pltpu
from jax.sharding import PartitionSpec as P

LANES = 128
MESH = pl.DeviceIdType.MESH
NT = (((1,), (1,)), ((), ()))
TN = (((0,), (0,)), ((), ()))
F32 = jnp.float32
BF16 = jnp.bfloat16


def dot(a, b, dims=(((1,), (0,)), ((), ()))):
    return lax.dot_general(a, b, dims, preferred_element_type=F32)


def onehot(rows, ids, base=0):
    at = lax.broadcasted_iota(jnp.int32, (rows, ids.shape[1]), 0).astype(jnp.int16)
    wanted = jnp.clip(ids - base, -1, rows).astype(jnp.int16)
    one = jnp.ones(at.shape, BF16)
    return jnp.where(at == wanted, one, jnp.zeros_like(one))


def onehot_rows(rows, ids_ref, first, count):
    return jnp.concatenate(
        [onehot(rows, ids_ref[pl.ds(first + j, 1), :]) for j in range(count)], axis=1
    )


def split(value):
    high = value.astype(BF16)
    low = (value - high.astype(F32)).astype(BF16)
    return jnp.concatenate([high, low], axis=0)


def joined(value):
    half = value.shape[0] // 2
    return value[:half] + value[half:]


def slots_of(owner_row, owners, padded):
    targets = owner_row.shape[1]
    lead = max(owners, 8)
    mine = onehot(lead, owner_row)
    earlier = lax.broadcasted_iota(jnp.int32, (targets, targets), 0)
    later = lax.broadcasted_iota(jnp.int32, (targets, targets), 1)
    before = dot(mine, (earlier < later).astype(BF16))
    rank = jnp.sum(before * mine.astype(F32), axis=0, keepdims=True)
    return owner_row * padded + rank.astype(jnp.int32)


def whole_kernel(
    count,
    owners,
    channels,
    factor,
    off_in,
    live,
    feat_in,
    ker_in,
    cg_in,
    pf_in,
    pt_in,
    own_in,
    slots_in,
    act_out,
    fine_out,
    weight_out,
    act,
    fine_here,
    feat,
    ker,
    cg,
    pf,
    pt,
    own,
    slots,
    off,
    routes,
    places,
    ft,
    foh,
    toh,
    gath,
    spread,
    send,
    recv,
    back,
    ret,
    prefix,
    links,
    acc,
    fsum,
    fsend,
    frecv,
    wsum,
    wnear,
    wpass,
    wfar,
    wfin,
    in_sem,
    end_sem,
    a_send,
    a_recv,
    b_send,
    b_recv,
    f_send,
    f_recv,
    near_send,
    near_recv,
    far_send,
    far_recv,
    out_send,
    out_recv,
    fwd_send,
    fwd_recv,
):
    fine_total, width_in = feat.shape
    offsets_all, width_out, _ = ker.shape
    targets = own.shape[1]
    coarse_total = cg.shape[1]
    padded = send.shape[2]
    blocks = pf.shape[0]
    groups = blocks // count
    slice_rows = wfin.shape[0] // owners
    outer = owners // 2
    vox = lax.axis_index("vox")
    ch = lax.axis_index("ch")
    mine_out, mine_in = vox // 2, lax.rem(vox, 2)

    barrier = pltpu.get_barrier_semaphore()
    for step in range(1, owners):
        pl.semaphore_signal(
            barrier, inc=1, device_id=(lax.rem(vox + step, owners), ch), device_id_type=MESH
        )
    for step in range(1, channels):
        pl.semaphore_signal(
            barrier, inc=1, device_id=(vox, lax.rem(ch + step, channels)), device_id_type=MESH
        )

    pairs = [
        (own_in, own),
        (slots_in, slots),
        (off_in, off),
        (pf_in, pf),
        (pt_in, pt),
        (feat_in, feat),
        (ker_in, ker),
        (cg_in, cg),
    ]
    loads = [pltpu.make_async_copy(a, b, in_sem.at[i]) for i, (a, b) in enumerate(pairs)]
    for load in loads:
        load.start()
    small = owners <= 16
    for load in loads[:2]:
        load.wait()
    slot = slots_of(own[...], owners, padded)
    if small:
        routes[...] = onehot(owners * padded, slot)
        capacity = slots.shape[0] * LANES // owners
        blank = jnp.full((1, padded - capacity), -1, jnp.int32)
        for o in range(owners):
            pieces, first = [], o * capacity
            while first < (o + 1) * capacity:
                row, lane = divmod(first, LANES)
                size = min(LANES - lane, (o + 1) * capacity - first)
                pieces.append(slots[row : row + 1, lane : lane + size])
                first += size
            if padded > capacity:
                pieces.append(blank)
            ids = jnp.concatenate(pieces, axis=1)
            places[:, o * padded : (o + 1) * padded] = onehot(coarse_total, ids)
    for load in loads[2:7]:
        load.wait()

    at = lax.broadcasted_iota(jnp.int32, (fine_total, width_in), 0)
    ft[...] = jnp.where(at < live[0], feat[...].astype(F32), 0.0).T.astype(BF16)

    def forward(g, total):
        foh[g] = onehot_rows(fine_total, pf, g * count, count)
        gathered = dot(ft[...], foh[g]).astype(BF16)
        gath[g] = gathered
        part = jnp.concatenate(
            [
                dot(ker[off[g * count + j]], gathered[:, j * LANES : (j + 1) * LANES])
                for j in range(count)
            ],
            axis=1,
        )
        toh[g] = onehot_rows(targets, pt, g * count, count)
        return total + dot(split(part), toh[g], NT)

    total = lax.fori_loop(
        0, groups, forward, jnp.zeros((2 * width_out, targets), F32), unroll=True
    )
    part = joined(total).astype(BF16)

    def route(o, carry):
        send[o] = dot(part, onehot(padded, slot, o * padded), NT).astype(BF16)
        return carry

    def apart(value, target):
        for o in range(owners):
            target[o] = value[:, o * padded : (o + 1) * padded].astype(BF16)

    def together(source):
        return jnp.concatenate([source[o] for o in range(owners)], axis=1)

    if small:
        apart(dot(part, routes[...], NT), send)
    else:
        lax.fori_loop(0, owners, route, 0)
    loads[7].wait()

    def exchange(source, target, out_sem, in_sem_of):
        copies = []
        for step in range(1, owners):
            to = lax.rem(vox + step, owners)
            copies.append(
                pltpu.make_async_remote_copy(
                    src_ref=source.at[to],
                    dst_ref=target.at[vox],
                    send_sem=out_sem.at[step],
                    recv_sem=in_sem_of.at[step],
                    device_id=(to, ch),
                    device_id_type=MESH,
                )
            )
            copies[-1].start()
        target[vox] = source[vox]
        return copies

    pl.semaphore_wait(barrier, owners - 1 + channels - 1)
    copies = exchange(send, recv, a_send, a_recv)

    def link(b, carry):
        found = jnp.int32(0)
        for other in range(blocks):
            same = jnp.logical_and(off[other] == off[b], other < b)
            found = jnp.where(same, jnp.int32(other + 1), found)
        links[b] = found
        return carry

    def ending(k, carry):
        found = jnp.int32(0)
        for other in range(blocks):
            found = jnp.where(off[other] == k, jnp.int32(other + 1), found)
        links[blocks + k] = found
        return carry

    lax.fori_loop(0, blocks, link, 0)
    for copy in copies:
        copy.wait()

    def gather(o, total):
        return total + dot(recv[o], onehot(coarse_total, slots[pl.ds(o, 1), :]), NT)

    if small:
        coarse = dot(together(recv), places[...], NT)
    else:
        coarse = lax.fori_loop(0, owners, gather, jnp.zeros(cg.shape, F32))
    gate = jax.nn.sigmoid(coarse)
    act[...] = (coarse * gate).astype(BF16)
    stores = [pltpu.make_async_copy(act, act_out, end_sem.at[0])]
    stores[-1].start()
    grad = (cg[...].astype(F32) * gate * (1.0 + coarse * (1.0 - gate))).astype(BF16)

    def give(o, carry):
        back[o] = dot(grad, onehot(coarse_total, slots[pl.ds(o, 1), :])).astype(BF16)
        return carry

    if small:
        apart(dot(grad, places[...]), back)
    else:
        lax.fori_loop(0, owners, give, 0)
    copies = exchange(back, ret, b_send, b_recv)
    prefix[0] = jnp.zeros_like(prefix[0])
    wsum[...] = jnp.zeros_like(wsum)
    lax.fori_loop(0, offsets_all, ending, 0)
    for copy in copies:
        copy.wait()

    def take(o, total):
        return total + dot(ret[o], onehot(padded, slot, o * padded))

    if small:
        grad = dot(together(ret), routes[...]).astype(BF16)
    else:
        grad = lax.fori_loop(
            0, owners, take, jnp.zeros((width_out, targets), F32)
        ).astype(BF16)

    def weigh(g, carry):
        rows = dot(grad, toh[g]).astype(BF16)
        spread[g] = rows
        gathered = gath[g]
        for j in range(count):
            lanes = slice(j * LANES, (j + 1) * LANES)
            b = g * count + j
            prefix[b + 1] = prefix[links[b]] + dot(rows[:, lanes], gathered[:, lanes], NT)
        return carry

    lax.fori_loop(0, groups, weigh, 0, unroll=True)

    def pick(k, carry):
        rows = pl.ds(pl.multiple_of(k * width_out, width_out), width_out)
        wsum[rows, :] = prefix[links[blocks + k]].astype(BF16)
        return carry

    lax.fori_loop(0, offsets_all, pick, 0, unroll=True)

    part_rows = wnear.shape[2]
    parts = slice_rows // part_rows

    def piece(out_at, in_at, part):
        first = (out_at * 2 + in_at) * slice_rows + part * part_rows
        return pl.ds(pl.multiple_of(first, 16), part_rows)

    partner = mine_out * 2 + 1 - mine_in
    order = list(range(1, outer)) + [0]
    near = {}
    for part in range(parts):
        for step in order:
            to = lax.rem(mine_out + step, outer)
            near[part, step] = pltpu.make_async_remote_copy(
                src_ref=wsum.at[piece(to, 1 - mine_in, part)],
                dst_ref=wnear.at[part, step],
                send_sem=near_send.at[part, step],
                recv_sem=near_recv.at[part, step],
                device_id=(partner, ch),
                device_id_type=MESH,
            )
            near[part, step].start()

    pace = 2 if groups % 2 == 0 else 1

    def scatter(turn):
        more = None
        for g in range(turn * pace, (turn + 1) * pace):
            terms = []
            for j in range(count):
                rows = spread[g, :, j * LANES : (j + 1) * LANES]
                terms.append(dot(ker[off[g * count + j]], rows, TN).astype(BF16))
            added = dot(jnp.concatenate(terms, axis=1), foh[g], NT)
            more = added if more is None else more + added
        acc[...] = more if turn == 0 else acc[...] + more

    far, totals = {}, {}

    def pass_on(part, step):
        to = lax.rem(mine_out + step, outer)
        near[part, step].wait()
        both = wsum[piece(to, mine_in, part), :].astype(F32)
        both = both + wnear[part, step].astype(F32)
        if step == 0:
            totals[part] = both
            return
        wpass[part, step] = both.astype(BF16)
        far[part, step] = pltpu.make_async_remote_copy(
            src_ref=wpass.at[part, step],
            dst_ref=wfar.at[part, step],
            send_sem=far_send.at[part, step],
            recv_sem=far_recv.at[part, step],
            device_id=(to * 2 + mine_in, ch),
            device_id_type=MESH,
        )
        far[part, step].start()

    turns = groups // pace
    scatter(0)
    for step in order[:-1]:
        pass_on(0, step)
    if turns > 1:
        scatter(1)
    pass_on(0, 0)
    for part in range(1, parts):
        for step in order:
            pass_on(part, step)
    for turn in range(2, turns - 1):
        scatter(turn)

    def finished(where, to, out_sem, in_sem_of):
        copy = pltpu.make_async_remote_copy(
            src_ref=wfin.at[where],
            dst_ref=wfin.at[where],
            send_sem=out_sem,
            recv_sem=in_sem_of,
            device_id=(to, ch),
            device_id_type=MESH,
        )
        copy.start()
        return copy

    outward, across = {}, []

    def finish(part):
        total = totals[part]
        for step in order[:-1]:
            far[part, step].wait()
            total = total + wfar[part, step].astype(F32)
        here = piece(mine_out, mine_in, part)
        wfin[here, :] = (total * factor).astype(BF16)
        for step in range(1, outer):
            outward[part, step] = finished(
                here,
                lax.rem(mine_out + step, outer) * 2 + mine_in,
                out_send.at[part, step],
                out_recv.at[part, step],
            )
        across.append(
            finished(here, partner, fwd_send.at[part, 0], fwd_recv.at[part, 0])
        )

    for part in range(parts):
        finish(part)
    if turns > 2:
        scatter(turns - 1)

    share = width_in // channels
    mask_at = lax.broadcasted_iota(jnp.int32, (width_in, fine_total), 1)
    whole = jnp.where(mask_at < live[0], acc[...], 0.0)
    fsum[...] = whole
    fsend[...] = whole.astype(BF16)
    fine = []
    for step in range(1, channels):
        to = lax.rem(ch + step, channels)
        fine.append(
            pltpu.make_async_remote_copy(
                src_ref=fsend.at[pl.ds(pl.multiple_of(to * share, share), share)],
                dst_ref=frecv.at[step],
                send_sem=f_send.at[step],
                recv_sem=f_recv.at[step],
                device_id=(vox, to),
                device_id_type=MESH,
            )
        )
        fine[-1].start()

    def forward_on(part):
        for step in range(1, outer):
            outward[part, step].wait()
            came = piece(lax.rem(mine_out + outer - step, outer), mine_in, part)
            across.append(
                finished(
                    came, partner, fwd_send.at[part, step], fwd_recv.at[part, step]
                )
            )

    forward_on(0)
    for copy in fine:
        copy.wait()
    kept = fsum[pl.ds(pl.multiple_of(ch * share, share), share), :]
    for step in range(1, channels):
        kept = kept + frecv[step].astype(F32)
    fine_here[...] = kept.astype(BF16)
    stores.append(pltpu.make_async_copy(fine_here, fine_out, end_sem.at[1]))
    stores[-1].start()
    for part in range(1, parts):
        forward_on(part)
    for copy in across:
        copy.wait()

    rows = offsets_all * width_out
    stores.append(
        pltpu.make_async_copy(wfin.at[pl.ds(0, rows)], weight_out, end_sem.at[2])
    )
    stores[-1].start()
    for copy in stores:
        copy.wait()


def write_kernel(a, b, c, a_out, b_out, c_out, a_mid, b_mid, c_mid, in_sem, out_sem):
    pairs = ((c, c_mid, c_out), (a, a_mid, a_out), (b, b_mid, b_out))
    loads = [pltpu.make_async_copy(p[0], p[1], in_sem.at[i]) for i, p in enumerate(pairs)]
    stores = [pltpu.make_async_copy(p[1], p[2], out_sem.at[i]) for i, p in enumerate(pairs)]
    for load in loads:
        load.start()
    for load, store in zip(loads, stores):
        load.wait()
        store.start()
    for store in stores:
        store.wait()


def body(
    features,
    kernel,
    coarse_grad,
    pair_fine,
    pair_target,
    block_offset,
    target_owner,
    slot_coarse_row,
    fine_count,
):
    owners = lax.axis_size("vox")
    channels = lax.axis_size("ch")
    fine_total, width_in = features.shape
    width_out, coarse_total = coarse_grad.shape
    offsets_all = kernel.shape[0]
    targets = target_owner.shape[0]
    capacity = slot_coarse_row.shape[0] // owners
    blocks = block_offset.shape[0]
    padded = -(-capacity // LANES) * LANES
    count = 4
    groups = blocks // count
    outer = owners // 2
    slice_rows = -(-offsets_all * width_out // (owners * 16)) * 16
    parts = 2 if slice_rows % 32 == 0 else 1
    share = width_in // channels
    hbm = pl.BlockSpec(memory_space=pltpu.HBM)
    pf = pair_fine.reshape(blocks, LANES)
    pt = pair_target.reshape(blocks, LANES)
    own = target_owner.reshape(1, targets)
    small = owners <= 16
    if small:
        slots = slot_coarse_row.reshape(-1, LANES)
    else:
        slots = jnp.pad(
            slot_coarse_row.reshape(owners, capacity),
            ((0, 0), (0, padded - capacity)),
            constant_values=-1,
        )
    kept = owners * padded if small else LANES
    factor = math.sqrt(offsets_all / (blocks * LANES * owners))
    operands = (features, kernel, coarse_grad, pf, pt, own, slots)
    wide = count * LANES
    dma = pltpu.SemaphoreType.DMA
    shapes = (
        jax.ShapeDtypeStruct((width_out, coarse_total), BF16),
        jax.ShapeDtypeStruct((share, fine_total), BF16),
        jax.ShapeDtypeStruct(kernel.shape, BF16),
    )
    scratch = [pltpu.VMEM(a.shape, BF16) for a in shapes[:2]]
    scratch += [pltpu.VMEM(a.shape, a.dtype) for a in operands] + [
        pltpu.SMEM(block_offset.shape, jnp.int32),
        pltpu.VMEM((kept, targets), BF16),
        pltpu.VMEM((coarse_total, kept), BF16),
        pltpu.VMEM((width_in, fine_total), BF16),
        pltpu.VMEM((groups, fine_total, wide), BF16),
        pltpu.VMEM((groups, targets, wide), BF16),
        pltpu.VMEM((groups, width_in, wide), BF16),
        pltpu.VMEM((groups, width_out, wide), BF16),
        pltpu.VMEM((owners, width_out, padded), BF16),
        pltpu.VMEM((owners, width_out, padded), BF16),
        pltpu.VMEM((owners, width_out, padded), BF16),
        pltpu.VMEM((owners, width_out, padded), BF16),
        pltpu.VMEM((blocks + 1, width_out, width_in), F32),
        pltpu.SMEM((blocks + offsets_all,), jnp.int32),
        pltpu.VMEM((width_in, fine_total), F32),
        pltpu.VMEM((width_in, fine_total), F32),
        pltpu.VMEM((width_in, fine_total), BF16),
        pltpu.VMEM((channels, share, fine_total), BF16),
        pltpu.VMEM((owners * slice_rows, width_in), BF16),
        pltpu.VMEM((parts, outer, slice_rows // parts, width_in), BF16),
        pltpu.VMEM((parts, outer, slice_rows // parts, width_in), BF16),
        pltpu.VMEM((parts, outer, slice_rows // parts, width_in), BF16),
        pltpu.VMEM((owners * slice_rows, width_in), BF16),
        dma((len(operands) + 1,)),
        dma((3,)),
        dma((owners,)),
        dma((owners,)),
        dma((owners,)),
        dma((owners,)),
        dma((channels,)),
        dma((channels,)),
    ] + [dma((parts, outer)) for _ in range(8)]
    results = pl.pallas_call(
        functools.partial(whole_kernel, count, owners, channels, factor),
        out_shape=shapes[:2]
        + (jax.ShapeDtypeStruct((offsets_all * width_out, width_in), BF16),),
        in_specs=[hbm, pl.BlockSpec(memory_space=pltpu.SMEM)] + [hbm] * len(operands),
        out_specs=(hbm, hbm, hbm),
        scratch_shapes=scratch,
        compiler_params=pltpu.CompilerParams(
            collective_id=0, has_side_effects=True, vmem_limit_bytes=60 * 2**20
        ),
    )(block_offset, fine_count, *operands)
    return pl.pallas_call(
        write_kernel,
        out_shape=shapes,
        in_specs=[hbm, hbm, hbm],
        out_specs=(hbm, hbm, hbm),
        scratch_shapes=[pltpu.VMEM(a.shape, BF16) for a in shapes] + [dma((3,)), dma((3,))],
        compiler_params=pltpu.CompilerParams(vmem_limit_bytes=60 * 2**20),
    )(results[0], results[1], results[2].reshape(kernel.shape))


def solution(mesh):
    in_specs = (
        P("vox", None),
        P(None, "ch", None),
        P("ch", "vox"),
        P("vox"),
        P("vox"),
        P("vox"),
        P("vox", None),
        P("vox"),
        P("vox"),
    )
    out_specs = (P("ch", "vox"), P("ch", "vox"), P(None, "ch", None))
    return jax.shard_map(body, mesh=mesh, in_specs=in_specs, out_specs=out_specs, check_vma=False)
```
